32 devices in a mesh: dom: 1, ep: 16 (over z, y, x), grp: 2 (over core).
Axes of the slice: x: 2, y: 2, z: 4, core: 2. Of those that a mesh axis runs over, the one named last changes fastest.
Arguments:
- hidden: bfloat16 [512, 7168], P(('dom', 'ep', 'grp')), may hold values from -6 to 6
- gain: float32 [7168], replicated, may hold values from 0.1 to 1.9
- router_w: bfloat16 [7168, 8], replicated, may hold values from -0.0625 to 0.0625
- routes: int32 [512, 4], P(('dom', 'ep', 'grp')), may hold values from 0 to 7, all different within a row; in each aligned block of 16 rows (0 to 15, 16 to 31, ...) at most 16 rows name the same one
- w_gate: bfloat16 [16, 2, 7168, 256], P('ep', 'grp'), may hold values from -0.0625 to 0.0625
- w_up: bfloat16 [16, 2, 7168, 256], P('ep', 'grp'), may hold values from -0.0625 to 0.0625
- w_down: bfloat16 [16, 2, 256, 7168], P('ep', 'grp'), may hold values from -0.1875 to 0.1875
Outputs:
- mixed: bfloat16 [512, 7168], P(('dom', 'ep', 'grp'))
The draws below stay inside these ranges and needn't reach their ends.
Inputs may be any that keep to these rules, and one draw needn't show every extreme that they name: `routes`: each token names 4 different experts; among the tokens of one device no expert is named by more than 16 tokens, a bound that some block reaches.
All inputs are finite; a program needn't handle non-finite values.
Results may differ from the reference program's by a relative error of at most 0.0072.
Values may be sent and summed in bfloat16 or wider, within the bound.
No kernel may reach another device: no remote copies, remote signals or barrier semaphores. Data moves between devices by JAX's collectives and lax.ppermute only.
A program may use at most 64 MiB of HBM per device.

```python
import math
import jax
import jax.numpy as jnp
import numpy as np
from jax import lax

D = 7168
HDEV = 256
SPLIT = 4
TOP = 4
TOK_DEV = 16
HID = 1024
E_GRP = 4
EXPERTS = 8
CAP = 16
TOKENS = 512
N_EP = 16
N_GRP = 2


def steps_of(stream_key, shape, cuts, smallest, top_value):
    level = 1.0
    for axis_at, blocks in cuts:
        steps = jax.random.uniform(jax.random.fold_in(jax.random.fold_in(stream_key, 6), axis_at), (blocks,), jnp.float32, smallest / len(cuts), top_value / len(cuts))
        level = level * jnp.repeat(jnp.exp(steps), shape[axis_at] // blocks).reshape((-1,) + (1,) * (len(shape) - 1 - axis_at))
    return level


def shared_out(own_key, own, number, rows, count, top, limit, skew):
    ranking = jax.random.permutation(own_key, count)
    heavy_load, common = load_shares(count, rows * top, limit, skew, True), load_shares(count, rows * top, limit, skew, False)
    places = jnp.arange(count)

    def named(sizes, rotation):
        used = int((sizes > 0).sum())
        fixed = max(1, used // 4)
        passed = fixed + (places - fixed + rotation * (used - fixed)) % max(1, count - fixed)
        return jnp.zeros((count,), jnp.int32).at[ranking[jnp.where(places < fixed, places, passed)]].set(jnp.asarray(sizes, jnp.int32))

    sizes = jnp.where(number % 4 == 0, named(heavy_load, number // 4), named(common, number - number // 4 - 1))
    mixed = jax.random.permutation(jax.random.fold_in(own, 3), count)
    source_of, receiver = mixed[0:count // 2 * 2:2], mixed[1:count // 2 * 2:2]
    slack = jnp.minimum(sizes[source_of] - 1, limit - sizes[receiver]) // 2
    slack = jnp.where((source_of == ranking[0]) | (receiver == ranking[0]) | (sizes[receiver] == 0), 0, jnp.maximum(slack, 0))
    passed = jax.random.randint(jax.random.fold_in(own, 4), (count // 2,), 0, 1 << 20) % (slack + 1)
    sizes = sizes.at[source_of].add(-passed).at[receiver].add(passed)
    labels = jnp.searchsorted(jnp.cumsum(sizes), jnp.arange(rows * top), side="right").astype(jnp.int32)
    grid = labels.reshape(top, rows).T
    grid = grid[jax.random.permutation(jax.random.fold_in(own, 1), rows)]
    rotation = jax.random.randint(jax.random.fold_in(own, 2), (rows, 1), 0, top)
    return jnp.take_along_axis(grid, (jnp.arange(top)[None, :] + rotation) % top, axis=1)


def load_shares(count, total, limit, slope, full):
    portions = [(1 << 20) // math.isqrt(grade ** slope) + 1 for grade in range(1, count + 1)]
    largest = limit if full else min(limit, max(-(-total // count), total * portions[0] // sum(portions)))
    least = 1 if total - largest >= count - 1 else 0
    given, rest = [largest] + [least] * (count - 1), total - largest - least * (count - 1)
    while rest > 0:
        candidates = [i for i in range(1, count) if given[i] < largest] or [i for i in range(1, count) if given[i] < limit]
        mass, remaining = sum([portions[i] for i in candidates]), rest
        for i in candidates:
            extra = min(limit - given[i], max(1, remaining * portions[i] // mass), rest)
            given[i] = given[i] + extra
            rest = rest - extra
    return np.array(given)


def centred(stream_key, shape, width, bound, shards=(), kind=jnp.bfloat16):
    drawn = jax.random.normal(stream_key, shape, jnp.float32) * width
    if len(shards) > 0:
        drawn = steps_of(stream_key, shape, shards, -0.22, 0.18) * drawn
    return jnp.clip(drawn, min=-bound, max=bound).astype(kind)


def setup_inputs(seed: int = 0, part: int = 0) -> dict:
    streams_of = jax.random.split(jax.random.key(seed), 8)
    part_splits = jax.random.split(jax.random.fold_in(streams_of[7], part), 8)
    hidden = centred(part_splits[0], (TOKENS, D), 1.0, 6.0, ((0, 32),))
    gain = jnp.clip(1.0 + 0.18 * jax.random.normal(streams_of[1], (D,), jnp.float32), 0.1, 1.9)
    router_w = centred(streams_of[2], (D, EXPERTS), D ** -0.5, 0.0625)
    routes_keys = jax.random.split(jax.random.fold_in(part_splits[3], 1), TOKENS // TOK_DEV)
    routes_turns = jax.random.permutation(jax.random.fold_in(part_splits[3], 3), TOKENS // TOK_DEV)
    routes = jax.vmap(lambda own, number: shared_out(jax.random.fold_in(part_splits[3], 2), own, number, TOK_DEV, EXPERTS, TOP, CAP, 2))(routes_keys, routes_turns).reshape((TOKENS, TOP))
    w_gate = centred(streams_of[4], (E_GRP * SPLIT, N_GRP, D, HDEV), D ** -0.5, 0.0625, ((0, 16), (1, 2)))
    w_up = centred(streams_of[5], (E_GRP * SPLIT, N_GRP, D, HDEV), D ** -0.5, 0.0625, ((0, 16), (1, 2)))
    w_down = centred(streams_of[6], (E_GRP * SPLIT, N_GRP, HDEV, D), HID ** -0.5, 0.1875, ((0, 16), (1, 2)))
    return {"hidden": hidden, "gain": gain, "router_w": router_w, "routes": routes, "w_gate": w_gate, "w_up": w_up, "w_down": w_down}


EPSILON = 1e-06
ROUTE_SCALE = 2.5

def normalize(hidden, gain):
    values = hidden.astype(jnp.float32)
    square_mean = lax.optimization_barrier(jnp.mean(values * values, axis=1, keepdims=True))
    return (values * lax.rsqrt(square_mean + EPSILON) * gain.astype(jnp.float32)[None, :]).astype(jnp.bfloat16)

def affinity_weights(normed, router_w, routes, expert_count):
    logits = jnp.dot(normed, router_w, preferred_element_type=jnp.float32)
    scores = jax.nn.sigmoid(logits)
    one_hot = (routes[:, :, None] == jnp.arange(expert_count, dtype=jnp.int32)[None, None, :]).astype(jnp.float32)
    chosen = lax.optimization_barrier(jnp.sum(one_hot * scores[:, None, :], axis=2))
    return (ROUTE_SCALE * chosen / lax.optimization_barrier(jnp.sum(chosen, axis=1, keepdims=True)), one_hot)

def reference(hidden, gain, router_w, routes, w_gate, w_up, w_down):
    normed = normalize(hidden, gain)
    weights, one_hot = affinity_weights(normed, router_w, routes, EXPERTS)
    coeffs = lax.optimization_barrier(jnp.sum(one_hot * weights[:, :, None], axis=1))
    owners = (jnp.arange(N_GRP, dtype=jnp.int32)[None, :] * (N_EP // SPLIT) + jnp.arange(N_EP, dtype=jnp.int32)[:, None] // SPLIT).reshape(-1).astype(jnp.int32)
    gate_all = w_gate.reshape(N_EP * N_GRP, D, HDEV)
    up_all = w_up.reshape(N_EP * N_GRP, D, HDEV)
    down_all = w_down.reshape(N_EP * N_GRP, HDEV, D)

    def add_slice(accum_sum, sliced):
        owner, gate_w, up_w, down_w = sliced
        gate_part = jnp.dot(normed, gate_w, preferred_element_type=jnp.float32)
        up_part = jnp.dot(normed, up_w, preferred_element_type=jnp.float32)
        activated = (jax.nn.silu(gate_part) * up_part).astype(jnp.bfloat16)
        partial_value = jnp.dot(activated, down_w, preferred_element_type=jnp.float32).astype(jnp.bfloat16)
        partial_value = lax.optimization_barrier(partial_value)
        column = lax.optimization_barrier(jnp.sum(coeffs * (jnp.arange(EXPERTS, dtype=jnp.int32)[None, :] == owner).astype(jnp.float32), axis=1))
        return (accum_sum + column[:, None] * partial_value.astype(jnp.float32), None)
    total, _ = lax.scan(add_slice, jnp.zeros((TOKENS, D), jnp.float32), (owners, gate_all, up_all, down_all))
    return total.astype(jnp.bfloat16)
```

```python
import jax
import jax.numpy as jnp
from jax import lax
from jax.sharding import PartitionSpec as P

SPLIT = 4
TOP = 4

EPSILON = 1e-06
ROUTE_SCALE = 2.5


def normalize(hidden, gain):
    values = hidden.astype(jnp.float32)
    square_mean = jnp.mean(values * values, axis=1, keepdims=True)
    return (values * lax.rsqrt(square_mean + EPSILON) * gain[None, :]).astype(jnp.bfloat16)


def expert_coeffs(normed, router_w, routes, expert_count):
    logits = jnp.dot(normed, router_w, preferred_element_type=jnp.float32)
    scores = jax.nn.sigmoid(logits)
    named = (routes[:, :, None] == jnp.arange(expert_count, dtype=jnp.int32)[None, None, :]).any(axis=1)
    chosen = jnp.where(named, scores, 0.0)
    return ROUTE_SCALE * chosen / jnp.sum(chosen, axis=1, keepdims=True)


def local(hidden, gain, router_w, routes, w_gate, w_up, w_down):
    ep_count = lax.axis_size("ep")
    grp_count = lax.axis_size("grp")
    local_experts = ep_count // SPLIT
    expert_count = local_experts * grp_count
    normed = normalize(hidden, gain)
    coeffs = expert_coeffs(normed, router_w, routes, expert_count)
    all_coeffs = lax.all_gather(coeffs, ("ep", "grp"), axis=0, tiled=True)
    tokens = lax.all_gather(normed, ("ep", "grp"), axis=0, tiled=True)
    owner = lax.axis_index("grp") * local_experts + lax.axis_index("ep") // SPLIT
    column = lax.dynamic_slice_in_dim(all_coeffs, owner, 1, axis=1)
    gate_part = jnp.dot(tokens, w_gate[0, 0], preferred_element_type=jnp.float32)
    up_part = jnp.dot(tokens, w_up[0, 0], preferred_element_type=jnp.float32)
    activated = (jax.nn.silu(gate_part) * up_part).astype(jnp.bfloat16)
    partial_value = jnp.dot(activated, w_down[0, 0], preferred_element_type=jnp.float32)
    weighted = (partial_value * column).astype(jnp.bfloat16)
    return lax.psum_scatter(weighted, ("ep", "grp"), scatter_dimension=0, tiled=True)


def solution(mesh):
    in_specs = (
        P(("dom", "ep", "grp"), None),
        P(),
        P(),
        P(("dom", "ep", "grp"), None),
        P("ep", "grp", None, None),
        P("ep", "grp", None, None),
        P("ep", "grp", None, None),
    )
    out_specs = P(("dom", "ep", "grp"), None)
    return jax.shard_map(local, mesh=mesh, in_specs=in_specs, out_specs=out_specs, check_vma=False)
```

```python
import functools

import jax
import jax.numpy as jnp
from jax import lax
from jax.experimental import pallas as pl
from jax.experimental.pallas import tpu as pltpu
from jax.sharding import PartitionSpec as P

SPLIT = 4
LANES = 128

EPSILON = 1e-06
ROUTE_SCALE = 2.5
VMEM_LIMIT = 56 * 1024 * 1024

TREE_16 = (
    (4, 4), (1, 1), (2, 2), (8, 8),
    (5, 1), (6, 2), (12, 4), (9, 1), (10, 2),
    (3, 1), (7, 2), (13, 4), (11, 1), (15, 2), (14, 4),
)


def gather_tree(ep_count):
    if ep_count == 16:
        return TREE_16
    return tuple((r, 1 << (r.bit_length() - 1)) for r in range(1, ep_count))


def across(value, bit, ep_count):
    return lax.ppermute(value, "ep", [(i, i ^ bit) for i in range(ep_count)])


def prepare_kernel(hidden_ref, gain_ref, routes_ref, out_ref):
    values = hidden_ref[...].astype(jnp.float32)
    width = values.shape[1]
    square_mean = jnp.mean(values * values, axis=1, keepdims=True)
    normed = values * lax.rsqrt(square_mean + EPSILON) * gain_ref[...]
    out_ref[:, :width] = normed.astype(jnp.bfloat16)
    routes = routes_ref[...]
    lanes = lax.broadcasted_iota(jnp.int32, (values.shape[0], LANES), 1)
    named = jnp.zeros((values.shape[0], LANES), jnp.float32)
    for k in range(routes.shape[1]):
        named = jnp.where(lanes == routes[:, k : k + 1], 1.0, named)
    out_ref[:, width:] = named.astype(jnp.bfloat16)


def prepare(hidden, gain, routes):
    rows, width = hidden.shape
    return pl.pallas_call(
        prepare_kernel,
        out_shape=jax.ShapeDtypeStruct((rows, width + LANES), jnp.bfloat16),
        compiler_params=pltpu.CompilerParams(vmem_limit_bytes=VMEM_LIMIT),
        cost_estimate=pl.CostEstimate(flops=6 * rows * width, bytes_accessed=4 * rows * width, transcendentals=rows),
        name="prepare",
    )(hidden, gain[None, :], routes)


def experts_kernel(blocks, k_steps, k_tile, ids_ref, *refs):
    token_refs = refs[:blocks]
    router_ref, gate0_ref, gate1_ref, up0_ref, up1_ref, down0_ref, down1_ref = refs[blocks : blocks + 7]
    out_refs = refs[blocks + 7 : 2 * blocks + 7]
    gates_ref, logits_ref, act_ref, coeff_ref = refs[2 * blocks + 7 :]
    step = pl.program_id(0)
    rows = token_refs[0].shape[0]
    hidden_units = gate0_ref.shape[1]
    width = k_steps * k_tile

    @pl.when(step < k_steps)
    def _():
        columns = pl.ds(pl.multiple_of(step * k_tile, LANES), k_tile)
        tokens = jnp.concatenate([ref[:, columns] for ref in token_refs], axis=0)
        parts = [
            jnp.dot(tokens, ref[...], preferred_element_type=jnp.float32)
            for ref in (gate0_ref, gate1_ref, up0_ref, up1_ref)
        ]
        logits = lax.dot_general(
            tokens, router_ref[...], (((1,), (1,)), ((), ())), preferred_element_type=jnp.float32
        )

        @pl.when(step == 0)
        def _():
            for i, part in enumerate(parts):
                gates_ref[:, i * hidden_units : (i + 1) * hidden_units] = part
            logits_ref[...] = logits

        @pl.when(step > 0)
        def _():
            for i, part in enumerate(parts):
                gates_ref[:, i * hidden_units : (i + 1) * hidden_units] += part
            logits_ref[...] += logits

    @pl.when(step == k_steps - 1)
    def _():
        gate_part = gates_ref[:, : 2 * hidden_units]
        up_part = gates_ref[:, 2 * hidden_units :]
        act_ref[...] = (jax.nn.silu(gate_part) * up_part).astype(jnp.bfloat16)
        named = jnp.concatenate([ref[:, width : width + LANES] for ref in token_refs], axis=0)
        experts = logits_ref.shape[1]
        scores = jax.nn.sigmoid(logits_ref[...])
        chosen = named[:, :experts].astype(jnp.float32) * scores
        weights = ROUTE_SCALE * chosen / jnp.sum(chosen, axis=1, keepdims=True)
        lanes = lax.broadcasted_iota(jnp.int32, weights.shape, 1)
        for i in range(2):
            column = jnp.sum(jnp.where(lanes == ids_ref[i], weights, 0.0), axis=1, keepdims=True)
            coeff_ref[:, i * LANES : (i + 1) * LANES] = jnp.broadcast_to(column, (column.shape[0], LANES))

    @pl.when(step >= k_steps)
    def _():
        total = coeff_ref[:, 0:1] * jnp.dot(
            act_ref[:, :hidden_units], down0_ref[...], preferred_element_type=jnp.float32
        ) + coeff_ref[:, LANES : LANES + 1] * jnp.dot(
            act_ref[:, hidden_units:], down1_ref[...], preferred_element_type=jnp.float32
        )
        for i, ref in enumerate(out_refs):
            ref[...] = total[i * rows : (i + 1) * rows].astype(jnp.bfloat16)


def experts(ids, token_blocks, router_t, gates, ups, downs):
    blocks = len(token_blocks)
    rows = token_blocks[0].shape[0]
    width, hidden_units = gates[0].shape
    k_tile = n_tile = 1024
    k_steps, n_steps = width // k_tile, width // n_tile
    all_rows = blocks * rows

    def at_k(step, ids_ref):
        return jnp.minimum(step, k_steps - 1)

    def at_n(step, ids_ref):
        return jnp.maximum(step - k_steps, 0)

    whole = pl.BlockSpec(token_blocks[0].shape, lambda step, ids_ref: (0, 0))
    in_specs = [whole] * blocks
    in_specs += [pl.BlockSpec((router_t.shape[0], k_tile), lambda step, ids_ref: (0, at_k(step, ids_ref)))]
    in_specs += [pl.BlockSpec((k_tile, hidden_units), lambda step, ids_ref: (at_k(step, ids_ref), 0))] * 4
    in_specs += [pl.BlockSpec((hidden_units, n_tile), lambda step, ids_ref: (0, at_n(step, ids_ref)))] * 2
    out_specs = [pl.BlockSpec((rows, n_tile), lambda step, ids_ref: (0, at_n(step, ids_ref)))] * blocks
    return pl.pallas_call(
        functools.partial(experts_kernel, blocks, k_steps, k_tile),
        grid_spec=pltpu.PrefetchScalarGridSpec(
            num_scalar_prefetch=1,
            grid=(k_steps + n_steps,),
            in_specs=in_specs,
            out_specs=out_specs,
            scratch_shapes=[
                pltpu.VMEM((all_rows, 4 * hidden_units), jnp.float32),
                pltpu.VMEM((all_rows, router_t.shape[0]), jnp.float32),
                pltpu.VMEM((all_rows, 2 * hidden_units), jnp.bfloat16),
                pltpu.VMEM((all_rows, 2 * LANES), jnp.float32),
            ],
        ),
        out_shape=[jax.ShapeDtypeStruct((rows, width), jnp.bfloat16)] * blocks,
        compiler_params=pltpu.CompilerParams(vmem_limit_bytes=VMEM_LIMIT),
        cost_estimate=pl.CostEstimate(
            flops=12 * all_rows * width * hidden_units,
            bytes_accessed=12 * width * hidden_units + 4 * all_rows * width,
            transcendentals=2 * all_rows * hidden_units,
        ),
        name="experts",
    )(ids, *token_blocks, router_t, *gates, *ups, *downs)


def local(hidden, gain, router_w, routes, w_gate, w_up, w_down):
    ep_count = lax.axis_size("ep")
    local_experts = ep_count // SPLIT
    expert_count = local_experts * lax.axis_size("grp")
    tree = gather_tree(ep_count)
    swap = [(0, 1), (1, 0)]
    own_weights = (w_gate[0, 0], w_up[0, 0], w_down[0, 0])
    other_weights = [lax.ppermute(w, "grp", swap) for w in own_weights]
    gates, ups, downs = zip(own_weights, other_weights)

    held = {0: prepare(hidden, gain, routes)}
    for r, bit in tree:
        held[r] = across(held[r ^ bit], bit, ep_count)

    place, core = lax.axis_index("ep") // SPLIT, lax.axis_index("grp")
    ids = jnp.stack([core * local_experts + place, (1 - core) * local_experts + place]).astype(jnp.int32)
    router_t = jnp.pad(router_w.T, ((0, -expert_count % 16), (0, 0)))
    parts = experts(ids, [held[r] for r in range(ep_count)], router_t, gates, ups, downs)

    arrived = {r: [] for r in range(ep_count)}

    def summed(r):
        total = parts[r].astype(jnp.float32)
        for value in arrived[r]:
            total = total + value.astype(jnp.float32)
        return total.astype(jnp.bfloat16)

    for r, bit in reversed(tree):
        arrived[r ^ bit].append(across(summed(r), bit, ep_count))
    return summed(0)


def solution(mesh):
    in_specs = (
        P(("dom", "ep", "grp"), None),
        P(),
        P(),
        P(("dom", "ep", "grp"), None),
        P("ep", "grp", None, None),
        P("ep", "grp", None, None),
        P("ep", "grp", None, None),
    )
    out_specs = P(("dom", "ep", "grp"), None)
    return jax.shard_map(local, mesh=mesh, in_specs=in_specs, out_specs=out_specs, check_vma=False)
```

```python
import functools

import jax
import jax.numpy as jnp
from jax import lax
from jax.experimental import pallas as pl
from jax.experimental.pallas import tpu as pltpu
from jax.sharding import PartitionSpec as P

SPLIT = 4
LANES = 128

EPSILON = 1e-06
ROUTE_SCALE = 2.5
PREPARE_VMEM = 4 * 1024 * 1024
EXPERTS_VMEM = 50 * 1024 * 1024

TREE_16 = (
    (8, 8), (2, 2), (4, 4), (1, 1), (3, 2),
    (12, 4), (9, 1), (10, 2), (6, 4), (13, 1),
    (14, 2), (11, 8), (7, 4), (5, 1), (15, 2),
)
OPEN = 5


def gather_tree(ep_count):
    if ep_count == 16:
        return TREE_16
    return tuple((r, 1 << (r.bit_length() - 1)) for r in range(1, ep_count))


def across(value, bit, ep_count):
    return lax.ppermute(value, "ep", [(i, i ^ bit) for i in range(ep_count)])


def prepare_kernel(hidden_ref, gain_ref, routes_ref, out_ref):
    values = hidden_ref[...].astype(jnp.float32)
    width = values.shape[1]
    square_mean = jnp.mean(values * values, axis=1, keepdims=True)
    normed = values * lax.rsqrt(square_mean + EPSILON) * gain_ref[...]
    out_ref[:, :width] = normed.astype(jnp.bfloat16)
    routes = routes_ref[...]
    lanes = lax.broadcasted_iota(jnp.int32, (values.shape[0], LANES), 1)
    named = jnp.zeros((values.shape[0], LANES), jnp.float32)
    for k in range(routes.shape[1]):
        named = jnp.where(lanes == routes[:, k : k + 1], 1.0, named)
    out_ref[:, width:] = named.astype(jnp.bfloat16)


def prepare(hidden, gain, routes):
    rows, width = hidden.shape
    return pl.pallas_call(
        prepare_kernel,
        out_shape=jax.ShapeDtypeStruct((rows, width + LANES), jnp.bfloat16),
        compiler_params=pltpu.CompilerParams(vmem_limit_bytes=PREPARE_VMEM),
        cost_estimate=pl.CostEstimate(flops=6 * rows * width, bytes_accessed=4 * rows * width, transcendentals=rows),
        name="prepare",
    )(hidden, gain[None, :], routes)


def experts_kernel(blocks, k_steps, k_tile, ids_ref, *refs):
    token_refs = refs[:blocks]
    router_ref, gate_ref, up_ref, down_ref = refs[blocks : blocks + 4]
    out_refs = refs[blocks + 4 : 2 * blocks + 4]
    gates_ref, logits_ref, act_ref, coeff_ref = refs[2 * blocks + 4 :]
    step = pl.program_id(0)
    rows = token_refs[0].shape[0]
    hidden_units = gate_ref.shape[2]
    width = k_steps * k_tile

    @pl.when(step < k_steps)
    def _():
        columns = pl.ds(pl.multiple_of(step * k_tile, LANES), k_tile)
        tokens = jnp.concatenate([ref[:, columns] for ref in token_refs], axis=0)
        parts = [
            jnp.dot(tokens, ref[i], preferred_element_type=jnp.float32)
            for ref in (gate_ref, up_ref)
            for i in range(2)
        ]
        logits = lax.dot_general(
            tokens, router_ref[...], (((1,), (1,)), ((), ())), preferred_element_type=jnp.float32
        )

        @pl.when(step == 0)
        def _():
            for i, part in enumerate(parts):
                gates_ref[:, i * hidden_units : (i + 1) * hidden_units] = part
            logits_ref[...] = logits

        @pl.when(step > 0)
        def _():
            for i, part in enumerate(parts):
                gates_ref[:, i * hidden_units : (i + 1) * hidden_units] += part
            logits_ref[...] += logits

    @pl.when(step == k_steps - 1)
    def _():
        gate_part = gates_ref[:, : 2 * hidden_units]
        up_part = gates_ref[:, 2 * hidden_units :]
        act_ref[...] = (jax.nn.silu(gate_part) * up_part).astype(jnp.bfloat16)
        named = jnp.concatenate([ref[:, width : width + LANES] for ref in token_refs], axis=0)
        experts = logits_ref.shape[1]
        scores = jax.nn.sigmoid(logits_ref[...])
        chosen = named[:, :experts].astype(jnp.float32) * scores
        weights = ROUTE_SCALE * chosen / jnp.sum(chosen, axis=1, keepdims=True)
        lanes = lax.broadcasted_iota(jnp.int32, weights.shape, 1)
        for i in range(2):
            column = jnp.sum(jnp.where(lanes == ids_ref[i], weights, 0.0), axis=1, keepdims=True)
            coeff_ref[:, i * LANES : (i + 1) * LANES] = jnp.broadcast_to(column, (column.shape[0], LANES))

    @pl.when(step >= k_steps)
    def _():
        total = coeff_ref[:, 0:1] * jnp.dot(
            act_ref[:, :hidden_units], down_ref[0], preferred_element_type=jnp.float32
        ) + coeff_ref[:, LANES : LANES + 1] * jnp.dot(
            act_ref[:, hidden_units:], down_ref[1], preferred_element_type=jnp.float32
        )
        for i, ref in enumerate(out_refs):
            ref[...] = total[i * rows : (i + 1) * rows].astype(jnp.bfloat16)


def experts(ids, token_blocks, router_t, gates, ups, downs):
    blocks = len(token_blocks)
    rows = token_blocks[0].shape[0]
    _, width, hidden_units = gates.shape
    k_tile = n_tile = width // 4
    k_steps, n_steps = width // k_tile, width // n_tile
    all_rows = blocks * rows

    def at_k(step, ids_ref):
        return jnp.minimum(step, k_steps - 1)

    def at_n(step, ids_ref):
        return jnp.maximum(step - k_steps, 0)

    whole = pl.BlockSpec(token_blocks[0].shape, lambda step, ids_ref: (0, 0))
    in_specs = [whole] * blocks
    in_specs += [pl.BlockSpec((router_t.shape[0], k_tile), lambda step, ids_ref: (0, at_k(step, ids_ref)))]
    in_specs += [pl.BlockSpec((2, k_tile, hidden_units), lambda step, ids_ref: (0, at_k(step, ids_ref), 0))] * 2
    in_specs += [pl.BlockSpec((2, hidden_units, n_tile), lambda step, ids_ref: (0, 0, at_n(step, ids_ref)))]
    out_specs = [pl.BlockSpec((rows, n_tile), lambda step, ids_ref: (0, at_n(step, ids_ref)))] * blocks
    return pl.pallas_call(
        functools.partial(experts_kernel, blocks, k_steps, k_tile),
        grid_spec=pltpu.PrefetchScalarGridSpec(
            num_scalar_prefetch=1,
            grid=(k_steps + n_steps,),
            in_specs=in_specs,
            out_specs=out_specs,
            scratch_shapes=[
                pltpu.VMEM((all_rows, 4 * hidden_units), jnp.float32),
                pltpu.VMEM((all_rows, router_t.shape[0]), jnp.float32),
                pltpu.VMEM((all_rows, 2 * hidden_units), jnp.bfloat16),
                pltpu.VMEM((all_rows, 2 * LANES), jnp.float32),
            ],
        ),
        out_shape=[jax.ShapeDtypeStruct((rows, width), jnp.bfloat16)] * blocks,
        compiler_params=pltpu.CompilerParams(vmem_limit_bytes=EXPERTS_VMEM),
        cost_estimate=pl.CostEstimate(
            flops=12 * all_rows * width * hidden_units,
            bytes_accessed=12 * width * hidden_units + 4 * all_rows * width,
            transcendentals=2 * all_rows * hidden_units,
        ),
        name="experts",
    )(ids, *token_blocks, router_t, gates, ups, downs)


def local(hidden, gain, router_w, routes, w_gate, w_up, w_down):
    ep_count = lax.axis_size("ep")
    local_experts = ep_count // SPLIT
    expert_count = local_experts * lax.axis_size("grp")
    tree = gather_tree(ep_count)
    gates, ups, downs = (lax.all_gather(w[0, 0], "grp") for w in (w_gate, w_up, w_down))

    held = {0: prepare(hidden, gain, routes)}
    for k, (r, bit) in enumerate(tree):
        block = held[r ^ bit]
        if k >= OPEN:
            block, _ = lax.optimization_barrier((block, held[tree[k - OPEN][0]]))
        held[r] = across(block, bit, ep_count)

    ids = (jnp.arange(2) * local_experts + lax.axis_index("ep") // SPLIT).astype(jnp.int32)
    router_t = jnp.pad(router_w.T, ((0, -expert_count % 16), (0, 0)))
    parts = experts(ids, [held[r] for r in range(ep_count)], router_t, gates, ups, downs)

    arrived = {r: [] for r in range(ep_count)}

    def summed(r):
        total = parts[r].astype(jnp.float32)
        for value in arrived[r]:
            total = total + value.astype(jnp.float32)
        return total.astype(jnp.bfloat16)

    for r, bit in reversed(tree):
        arrived[r ^ bit].append(across(summed(r), bit, ep_count))
    return summed(0)


def solution(mesh):
    in_specs = (
        P(("dom", "ep", "grp"), None),
        P(),
        P(),
        P(("dom", "ep", "grp"), None),
        P("ep", "grp", None, None),
        P("ep", "grp", None, None),
        P("ep", "grp", None, None),
    )
    out_specs = P(("dom", "ep", "grp"), None)
    return jax.shard_map(local, mesh=mesh, in_specs=in_specs, out_specs=out_specs, check_vma=False)
```

```python
import functools

import jax
import jax.numpy as jnp
from jax import lax
from jax.experimental import pallas as pl
from jax.experimental.pallas import tpu as pltpu
from jax.sharding import PartitionSpec as P

SPLIT = 4
LANES = 128

EPSILON = 1e-06
ROUTE_SCALE = 2.5
PREPARE_VMEM = 4 * 1024 * 1024
EXPERTS_VMEM = 44 * 1024 * 1024

PLAN_16 = ((0, 4, 8), (0, 1, 2), (1, 1, 2), (1, 2, 1), (2, 2, 0), (3, 8, 1), (3, 2, 4), (6, 1, 4))


def plan_for(ep_count, grp_count):
    if ep_count == 16 and grp_count == 2:
        return PLAN_16, True
    plan = []
    for r in range(1, ep_count):
        bit = 1 << (r.bit_length() - 1)
        plan.append((r ^ bit, bit, bit))
    return tuple(plan), False


def across(value, bits, ep_count):
    pairs = [(i * 2 + c, (i ^ bit) * 2 + c) for c, bit in enumerate(bits) if bit for i in range(ep_count)]
    return lax.ppermute(value, ("ep", "grp"), pairs)


def between_cores(value):
    return lax.ppermute(value, "grp", [(0, 1), (1, 0)])


def prepare_kernel(hidden_ref, gain_ref, routes_ref, out_ref):
    values = hidden_ref[...].astype(jnp.float32)
    width = values.shape[1]
    square_mean = jnp.mean(values * values, axis=1, keepdims=True)
    normed = values * lax.rsqrt(square_mean + EPSILON) * gain_ref[...]
    out_ref[:, :width] = normed.astype(jnp.bfloat16)
    routes = routes_ref[...]
    lanes = lax.broadcasted_iota(jnp.int32, (values.shape[0], LANES), 1)
    named = jnp.zeros((values.shape[0], LANES), jnp.float32)
    for k in range(routes.shape[1]):
        named = jnp.where(lanes == routes[:, k : k + 1], 1.0, named)
    out_ref[:, width:] = named.astype(jnp.bfloat16)


def prepare(hidden, gain, routes):
    rows, width = hidden.shape
    return pl.pallas_call(
        prepare_kernel,
        out_shape=jax.ShapeDtypeStruct((rows, width + LANES), jnp.bfloat16),
        compiler_params=pltpu.CompilerParams(vmem_limit_bytes=PREPARE_VMEM),
        cost_estimate=pl.CostEstimate(flops=6 * rows * width, bytes_accessed=4 * rows * width, transcendentals=rows),
        name="prepare",
    )(hidden, gain[None, :], routes)


def experts_kernel(blocks, k_steps, k_tile, ids_ref, *refs):
    token_refs = refs[:blocks]
    router_ref, gate0_ref, gate1_ref, up0_ref, up1_ref, down0_ref, down1_ref = refs[blocks : blocks + 7]
    out_refs = refs[blocks + 7 : 2 * blocks + 7]
    gates_ref, logits_ref, act_ref, coeff_ref = refs[2 * blocks + 7 :]
    step = pl.program_id(0)
    rows = token_refs[0].shape[0]
    hidden_units = gate0_ref.shape[1]
    width = k_steps * k_tile

    @pl.when(step < k_steps)
    def _():
        columns = pl.ds(pl.multiple_of(step * k_tile, LANES), k_tile)
        tokens = jnp.concatenate([ref[:, columns] for ref in token_refs], axis=0)
        parts = [
            jnp.dot(tokens, ref[...], preferred_element_type=jnp.float32)
            for ref in (gate0_ref, gate1_ref, up0_ref, up1_ref)
        ]
        logits = lax.dot_general(
            tokens, router_ref[...], (((1,), (1,)), ((), ())), preferred_element_type=jnp.float32
        )

        @pl.when(step == 0)
        def _():
            for i, part in enumerate(parts):
                gates_ref[:, i * hidden_units : (i + 1) * hidden_units] = part
            logits_ref[...] = logits

        @pl.when(step > 0)
        def _():
            for i, part in enumerate(parts):
                gates_ref[:, i * hidden_units : (i + 1) * hidden_units] += part
            logits_ref[...] += logits

    @pl.when(step == k_steps - 1)
    def _():
        gate_part = gates_ref[:, : 2 * hidden_units]
        up_part = gates_ref[:, 2 * hidden_units :]
        act_ref[...] = (jax.nn.silu(gate_part) * up_part).astype(jnp.bfloat16)
        named = jnp.concatenate([ref[:, width : width + LANES] for ref in token_refs], axis=0)
        experts = logits_ref.shape[1]
        scores = jax.nn.sigmoid(logits_ref[...])
        chosen = named[:, :experts].astype(jnp.float32) * scores
        weights = ROUTE_SCALE * chosen / jnp.sum(chosen, axis=1, keepdims=True)
        lanes = lax.broadcasted_iota(jnp.int32, weights.shape, 1)
        for i in range(2):
            column = jnp.sum(jnp.where(lanes == ids_ref[i], weights, 0.0), axis=1, keepdims=True)
            coeff_ref[:, i * LANES : (i + 1) * LANES] = jnp.broadcast_to(column, (column.shape[0], LANES))

    @pl.when(step >= k_steps)
    def _():
        total = coeff_ref[:, 0:1] * jnp.dot(
            act_ref[:, :hidden_units], down0_ref[...], preferred_element_type=jnp.float32
        ) + coeff_ref[:, LANES : LANES + 1] * jnp.dot(
            act_ref[:, hidden_units:], down1_ref[...], preferred_element_type=jnp.float32
        )
        for i, ref in enumerate(out_refs):
            ref[...] = total[i * rows : (i + 1) * rows].astype(jnp.bfloat16)


def experts(ids, token_blocks, router_t, gates, ups, downs):
    blocks = len(token_blocks)
    rows = token_blocks[0].shape[0]
    width, hidden_units = gates[0].shape
    k_tile = n_tile = width // 4
    k_steps, n_steps = width // k_tile, width // n_tile
    all_rows = blocks * rows

    def at_k(step, ids_ref):
        return jnp.minimum(step, k_steps - 1)

    def at_n(step, ids_ref):
        return jnp.maximum(step - k_steps, 0)

    whole = pl.BlockSpec(token_blocks[0].shape, lambda step, ids_ref: (0, 0))
    in_specs = [whole] * blocks
    in_specs += [pl.BlockSpec((router_t.shape[0], k_tile), lambda step, ids_ref: (0, at_k(step, ids_ref)))]
    in_specs += [pl.BlockSpec((k_tile, hidden_units), lambda step, ids_ref: (at_k(step, ids_ref), 0))] * 4
    in_specs += [pl.BlockSpec((hidden_units, n_tile), lambda step, ids_ref: (0, at_n(step, ids_ref)))] * 2
    out_specs = [pl.BlockSpec((rows, n_tile), lambda step, ids_ref: (0, at_n(step, ids_ref)))] * blocks
    return pl.pallas_call(
        functools.partial(experts_kernel, blocks, k_steps, k_tile),
        grid_spec=pltpu.PrefetchScalarGridSpec(
            num_scalar_prefetch=1,
            grid=(k_steps + n_steps,),
            in_specs=in_specs,
            out_specs=out_specs,
            scratch_shapes=[
                pltpu.VMEM((all_rows, 4 * hidden_units), jnp.float32),
                pltpu.VMEM((all_rows, router_t.shape[0]), jnp.float32),
                pltpu.VMEM((all_rows, 2 * hidden_units), jnp.bfloat16),
                pltpu.VMEM((all_rows, 2 * LANES), jnp.float32),
            ],
        ),
        out_shape=[jax.ShapeDtypeStruct((rows, width), jnp.bfloat16)] * blocks,
        compiler_params=pltpu.CompilerParams(vmem_limit_bytes=EXPERTS_VMEM),
        cost_estimate=pl.CostEstimate(
            flops=12 * all_rows * width * hidden_units,
            bytes_accessed=12 * width * hidden_units + 4 * all_rows * width,
            transcendentals=2 * all_rows * hidden_units,
        ),
        name="experts",
    )(ids, *token_blocks, router_t, *gates, *ups, *downs)


def local(hidden, gain, router_w, routes, w_gate, w_up, w_down):
    ep_count, grp_count = lax.axis_size("ep"), lax.axis_size("grp")
    local_experts = ep_count // SPLIT
    expert_count = local_experts * grp_count
    place, core = lax.axis_index("ep") // SPLIT, lax.axis_index("grp")
    plan, paired = plan_for(ep_count, grp_count)
    rows = hidden.shape[0]
    gates, ups, downs = ((w[0, 0], between_cores(w[0, 0])) for w in (w_gate, w_up, w_down))

    own = prepare(hidden, gain, routes)
    if paired:
        own = jnp.concatenate([own, between_cores(own)], axis=0)
    held = [own]
    for parent, *bits in plan:
        held.append(across(held[parent], bits, ep_count))
    first = 0
    if paired:
        first = 1
        spare = [0 in bits for _, *bits in plan].index(True) + 1
        held[spare] = jnp.where(core == 1, own, held[spare])

    ids = jnp.stack([core * local_experts + place, (1 - core) * local_experts + place]).astype(jnp.int32)
    router_t = jnp.pad(router_w.T, ((0, -expert_count % 16), (0, 0)))
    parts = experts(ids, held[first:], router_t, gates, ups, downs)

    terms = [[] for _ in range(first)] + [[part] for part in parts]
    if paired:
        terms[0].append(jnp.where(core == 1, parts[spare - 1], jnp.zeros_like(parts[spare - 1])))

    def summed(slot):
        return sum(term.astype(jnp.float32) for term in terms[slot])

    for slot in range(len(plan), 0, -1):
        parent, *bits = plan[slot - 1]
        terms[parent].append(across(summed(slot).astype(jnp.bfloat16), bits, ep_count))
    total = summed(0)
    if paired:
        arrived = between_cores(total[rows:].astype(jnp.bfloat16))
        total = total[:rows] + arrived.astype(jnp.float32)
    return total.astype(jnp.bfloat16)


def solution(mesh):
    in_specs = (
        P(("dom", "ep", "grp"), None),
        P(),
        P(),
        P(("dom", "ep", "grp"), None),
        P("ep", "grp", None, None),
        P("ep", "grp", None, None),
        P("ep", "grp", None, None),
    )
    out_specs = P(("dom", "ep", "grp"), None)
    return jax.shard_map(local, mesh=mesh, in_specs=in_specs, out_specs=out_specs, check_vma=False)
```

```python
import functools

import jax
import jax.numpy as jnp
from jax import lax
from jax.experimental import pallas as pl
from jax.experimental.pallas import tpu as pltpu
from jax.sharding import PartitionSpec as P

SPLIT = 4
LANES = 128

EPSILON = 1e-06
ROUTE_SCALE = 2.5
PREPARE_VMEM = 4 * 1024 * 1024
EXPERTS_VMEM = 44 * 1024 * 1024

PLAN_16 = ((0, 4, 8), (0, 2, 1), (1, 2, 1), (1, 8, 2), (3, 1, 4), (1, 1, 0), (4, 2, 1), (5, 4, 2))
RETURN_16 = (6, 8, 7, 5, 4, 3, 1, 2)
OPEN_16 = (2, 2, 2, 2, 2, 3, 4, 4)
WEIGHTS_END_16 = {6: 0, 7: 1}
OPEN_RETURN = 4


def plan_for(ep_count, grp_count):
    if ep_count == 16 and grp_count == 2:
        return PLAN_16, RETURN_16, OPEN_16, WEIGHTS_END_16, True
    plan = []
    for r in range(1, ep_count):
        bit = 1 << (r.bit_length() - 1)
        plan.append((r ^ bit, bit, bit))
    slots = len(plan)
    return tuple(plan), tuple(range(slots, 0, -1)), (OPEN_RETURN,) * slots, {}, False


def across(value, bits, ep_count):
    pairs = [(i * 2 + c, (i ^ bit) * 2 + c) for c, bit in enumerate(bits) if bit for i in range(ep_count)]
    return lax.ppermute(value, ("ep", "grp"), pairs)


def after(value, earlier):
    return lax.optimization_barrier((value, *earlier))[0] if earlier else value


def between_cores(value):
    return lax.ppermute(value, "grp", [(0, 1), (1, 0)])


def prepare_kernel(hidden_ref, gain_ref, routes_ref, out_ref):
    values = hidden_ref[...].astype(jnp.float32)
    width = values.shape[1]
    square_mean = jnp.mean(values * values, axis=1, keepdims=True)
    normed = values * lax.rsqrt(square_mean + EPSILON) * gain_ref[...]
    out_ref[:, :width] = normed.astype(jnp.bfloat16)
    rows = values.shape[0]
    routes = routes_ref[...]
    experts_down = lax.broadcasted_iota(jnp.int32, (LANES, rows), 0)
    named = jnp.zeros((LANES, rows), jnp.float32)
    for k in range(routes.shape[0]):
        named = jnp.where(experts_down == routes[k : k + 1, :], 1.0, named)
    same = lax.broadcasted_iota(jnp.int32, (rows, rows), 0) == lax.broadcasted_iota(jnp.int32, (rows, rows), 1)
    out_ref[:, width:] = lax.dot_general(
        same.astype(jnp.bfloat16),
        named.astype(jnp.bfloat16),
        (((1,), (1,)), ((), ())),
        preferred_element_type=jnp.float32,
    ).astype(jnp.bfloat16)


def prepare(hidden, gain, routes):
    rows, width = hidden.shape
    return pl.pallas_call(
        prepare_kernel,
        out_shape=jax.ShapeDtypeStruct((rows, width + LANES), jnp.bfloat16),
        compiler_params=pltpu.CompilerParams(vmem_limit_bytes=PREPARE_VMEM),
        cost_estimate=pl.CostEstimate(flops=6 * rows * width, bytes_accessed=4 * rows * width, transcendentals=rows),
        name="prepare",
    )(hidden, gain[None, :], routes.T)


def experts_kernel(blocks, k_steps, k_tile, ids_ref, *refs):
    token_refs = refs[:blocks]
    router_ref, gate0_ref, gate1_ref, up0_ref, up1_ref, down0_ref, down1_ref = refs[blocks : blocks + 7]
    out_refs = refs[blocks + 7 : 2 * blocks + 7]
    gates_ref, logits_ref, act_ref, coeff_ref = refs[2 * blocks + 7 :]
    step = pl.program_id(0)
    rows = token_refs[0].shape[0]
    hidden_units = gate0_ref.shape[1]
    width = k_steps * k_tile

    @pl.when(step < k_steps)
    def _():
        columns = pl.ds(pl.multiple_of(step * k_tile, LANES), k_tile)
        tokens = jnp.concatenate([ref[:, columns] for ref in token_refs], axis=0)
        parts = [
            jnp.dot(tokens, ref[...], preferred_element_type=jnp.float32)
            for ref in (gate0_ref, gate1_ref, up0_ref, up1_ref)
        ]
        logits = lax.dot_general(
            tokens, router_ref[...], (((1,), (1,)), ((), ())), preferred_element_type=jnp.float32
        )

        @pl.when(step == 0)
        def _():
            for i, part in enumerate(parts):
                gates_ref[:, i * hidden_units : (i + 1) * hidden_units] = part
            logits_ref[...] = logits

        @pl.when(step > 0)
        def _():
            for i, part in enumerate(parts):
                gates_ref[:, i * hidden_units : (i + 1) * hidden_units] += part
            logits_ref[...] += logits

    @pl.when(step == k_steps - 1)
    def _():
        gate_part = gates_ref[:, : 2 * hidden_units]
        up_part = gates_ref[:, 2 * hidden_units :]
        act_ref[...] = (jax.nn.silu(gate_part) * up_part).astype(jnp.bfloat16)
        named = jnp.concatenate([ref[:, width : width + LANES] for ref in token_refs], axis=0)
        experts = logits_ref.shape[1]
        scores = jax.nn.sigmoid(logits_ref[...])
        chosen = named[:, :experts].astype(jnp.float32) * scores
        weights = ROUTE_SCALE * chosen / jnp.sum(chosen, axis=1, keepdims=True)
        lanes = lax.broadcasted_iota(jnp.int32, weights.shape, 1)
        for i in range(2):
            column = jnp.sum(jnp.where(lanes == ids_ref[i], weights, 0.0), axis=1, keepdims=True)
            coeff_ref[:, i * LANES : (i + 1) * LANES] = jnp.broadcast_to(column, (column.shape[0], LANES))

    @pl.when(step >= k_steps)
    def _():
        total = coeff_ref[:, 0:1] * jnp.dot(
            act_ref[:, :hidden_units], down0_ref[...], preferred_element_type=jnp.float32
        ) + coeff_ref[:, LANES : LANES + 1] * jnp.dot(
            act_ref[:, hidden_units:], down1_ref[...], preferred_element_type=jnp.float32
        )
        for i, ref in enumerate(out_refs):
            ref[...] = total[i * rows : (i + 1) * rows].astype(jnp.bfloat16)


def experts(ids, token_blocks, router_t, gates, ups, downs):
    blocks = len(token_blocks)
    rows = token_blocks[0].shape[0]
    width, hidden_units = gates[0].shape
    k_tile = n_tile = width // 4
    k_steps, n_steps = width // k_tile, width // n_tile
    all_rows = blocks * rows

    def at_k(step, ids_ref):
        return jnp.minimum(step, k_steps - 1)

    def at_n(step, ids_ref):
        return jnp.maximum(step - k_steps, 0)

    whole = pl.BlockSpec(token_blocks[0].shape, lambda step, ids_ref: (0, 0))
    in_specs = [whole] * blocks
    in_specs += [pl.BlockSpec((router_t.shape[0], k_tile), lambda step, ids_ref: (0, at_k(step, ids_ref)))]
    in_specs += [pl.BlockSpec((k_tile, hidden_units), lambda step, ids_ref: (at_k(step, ids_ref), 0))] * 4
    in_specs += [pl.BlockSpec((hidden_units, n_tile), lambda step, ids_ref: (0, at_n(step, ids_ref)))] * 2
    out_specs = [pl.BlockSpec((rows, n_tile), lambda step, ids_ref: (0, at_n(step, ids_ref)))] * blocks
    return pl.pallas_call(
        functools.partial(experts_kernel, blocks, k_steps, k_tile),
        grid_spec=pltpu.PrefetchScalarGridSpec(
            num_scalar_prefetch=1,
            grid=(k_steps + n_steps,),
            in_specs=in_specs,
            out_specs=out_specs,
            scratch_shapes=[
                pltpu.VMEM((all_rows, 4 * hidden_units), jnp.float32),
                pltpu.VMEM((all_rows, router_t.shape[0]), jnp.float32),
                pltpu.VMEM((all_rows, 2 * hidden_units), jnp.bfloat16),
                pltpu.VMEM((all_rows, 2 * LANES), jnp.float32),
            ],
        ),
        out_shape=[jax.ShapeDtypeStruct((rows, width), jnp.bfloat16)] * blocks,
        compiler_params=pltpu.CompilerParams(vmem_limit_bytes=EXPERTS_VMEM),
        cost_estimate=pl.CostEstimate(
            flops=12 * all_rows * width * hidden_units,
            bytes_accessed=12 * width * hidden_units + 4 * all_rows * width,
            transcendentals=2 * all_rows * hidden_units,
        ),
        name="experts",
    )(ids, *token_blocks, router_t, *gates, *ups, *downs)


def local(hidden, gain, router_w, routes, w_gate, w_up, w_down):
    ep_count, grp_count = lax.axis_size("ep"), lax.axis_size("grp")
    local_experts = ep_count // SPLIT
    expert_count = local_experts * grp_count
    place, core = lax.axis_index("ep") // SPLIT, lax.axis_index("grp")
    plan, return_order, most_open, weights_end, paired = plan_for(ep_count, grp_count)
    rows = hidden.shape[0]
    weights = [(w[0, 0], between_cores(w[0, 0])) for w in (w_gate, w_up, w_down)]

    own = prepare(hidden, gain, routes)
    if paired:
        own = jnp.concatenate([own, between_cores(own)], axis=0)
    held = [own]
    for slot, (parent, *bits) in enumerate(plan, 1):
        ended = held[1 : slot + 1 - most_open[slot - 1]]
        if slot in weights_end:
            ended.append(weights[weights_end[slot]][1])
        held.append(across(after(held[parent], ended), bits, ep_count))
    first = 0
    if paired:
        first = 1
        spare = [0 in bits for _, *bits in plan].index(True) + 1
        held[spare] = jnp.where(core == 1, own, held[spare])

    ids = jnp.stack([core * local_experts + place, (1 - core) * local_experts + place]).astype(jnp.int32)
    router_t = jnp.pad(router_w.T, ((0, -expert_count % 16), (0, 0)))
    parts = experts(ids, held[first:], router_t, *weights)

    terms = [[] for _ in range(first)] + [[part] for part in parts]
    if paired:
        terms[0].append(jnp.where(core == 1, parts[spare - 1], jnp.zeros_like(parts[spare - 1])))

    def summed(slot):
        return sum(term.astype(jnp.float32) for term in terms[slot])

    returned = []
    for slot in return_order:
        parent, *bits = plan[slot - 1]
        value = after(summed(slot).astype(jnp.bfloat16), returned[: max(0, len(returned) + 1 - OPEN_RETURN)])
        returned.append(across(value, bits, ep_count))
        terms[parent].append(returned[-1])
    total = summed(0)
    if paired:
        arrived = between_cores(total[rows:].astype(jnp.bfloat16))
        total = total[:rows] + arrived.astype(jnp.float32)
    return total.astype(jnp.bfloat16)


def solution(mesh):
    in_specs = (
        P(("dom", "ep", "grp"), None),
        P(),
        P(),
        P(("dom", "ep", "grp"), None),
        P("ep", "grp", None, None),
        P("ep", "grp", None, None),
        P("ep", "grp", None, None),
    )
    out_specs = P(("dom", "ep", "grp"), None)
    return jax.shard_map(local, mesh=mesh, in_specs=in_specs, out_specs=out_specs, check_vma=False)
```

```python
import functools

import jax
import jax.numpy as jnp
from jax import lax
from jax.experimental import pallas as pl
from jax.experimental.pallas import tpu as pltpu
from jax.sharding import PartitionSpec as P

SPLIT = 4
LANES = 128

EPSILON = 1e-06
ROUTE_SCALE = 2.5
PREPARE_VMEM = 60 * 1024 * 1024
EXPERTS_VMEM = 44 * 1024 * 1024

PLAN_16 = ((0, 8, 2), (0, 4, 1), (1, 2, 1), (1, 1, 4), (4, 2, 8), (4, 4, 1), (5, 4, 2), (2, 1, 0))
RETURN_16 = (7, 8, 6, 5, 2, 4, 3, 1)
OPEN_16 = (2, 2, 2, 2, 2, 3, 4, 4)
WEIGHTS_END_16 = {6: 0, 7: 1}
OPEN_RETURN = 4


def plan_for(ep_count, grp_count):
    if ep_count == 16 and grp_count == 2:
        return PLAN_16, RETURN_16, OPEN_16, WEIGHTS_END_16, True
    plan = []
    for r in range(1, ep_count):
        bit = 1 << (r.bit_length() - 1)
        plan.append((r ^ bit, bit, bit))
    slots = len(plan)
    return tuple(plan), tuple(range(slots, 0, -1)), (OPEN_RETURN,) * slots, {}, False


def across(value, bits, ep_count):
    pairs = [(i * 2 + c, (i ^ bit) * 2 + c) for c, bit in enumerate(bits) if bit for i in range(ep_count)]
    return lax.ppermute(value, ("ep", "grp"), pairs)


def after(value, earlier):
    return lax.optimization_barrier((value, *earlier))[0] if earlier else value


def between_cores(value):
    return lax.ppermute(value, "grp", [(0, 1), (1, 0)])


def prepare_kernel(hidden_hbm, gain_hbm, routes_hbm, out_ref, hidden_ref, gain_ref, routes_ref, sems):
    copies = [
        pltpu.make_async_copy(source, target, sems.at[i])
        for i, (source, target) in enumerate(
            ((hidden_hbm, hidden_ref), (gain_hbm, gain_ref), (routes_hbm, routes_ref))
        )
    ]
    for copy in copies:
        copy.start()
    for copy in copies:
        copy.wait()
    values = hidden_ref[...].astype(jnp.float32)
    width = values.shape[1]
    square_mean = jnp.mean(values * values, axis=1, keepdims=True)
    normed = values * lax.rsqrt(square_mean + EPSILON) * gain_ref[...]
    out_ref[:, :width] = normed.astype(jnp.bfloat16)
    rows = values.shape[0]
    routes = routes_ref[...]
    experts_down = lax.broadcasted_iota(jnp.int32, (LANES, rows), 0)
    named = jnp.zeros((LANES, rows), jnp.float32)
    for k in range(routes.shape[0]):
        named = jnp.where(experts_down == routes[k : k + 1, :], 1.0, named)
    same = lax.broadcasted_iota(jnp.int32, (rows, rows), 0) == lax.broadcasted_iota(jnp.int32, (rows, rows), 1)
    out_ref[:, width:] = lax.dot_general(
        same.astype(jnp.bfloat16),
        named.astype(jnp.bfloat16),
        (((1,), (1,)), ((), ())),
        preferred_element_type=jnp.float32,
    ).astype(jnp.bfloat16)


def prepare(hidden, gain, routes):
    rows, width = hidden.shape
    return pl.pallas_call(
        prepare_kernel,
        out_shape=jax.ShapeDtypeStruct((rows, width + LANES), jnp.bfloat16),
        in_specs=[pl.BlockSpec(memory_space=pltpu.HBM)] * 3,
        scratch_shapes=[
            pltpu.VMEM(hidden.shape, jnp.bfloat16),
            pltpu.VMEM((1, width), jnp.float32),
            pltpu.VMEM(routes.shape[::-1], jnp.int32),
            pltpu.SemaphoreType.DMA((3,)),
        ],
        compiler_params=pltpu.CompilerParams(vmem_limit_bytes=PREPARE_VMEM),
        cost_estimate=pl.CostEstimate(flops=6 * rows * width, bytes_accessed=4 * rows * width, transcendentals=rows),
        name="prepare",
    )(hidden, gain[None, :], routes.T)


def experts_kernel(blocks, n_tile, ids_ref, router_ref, *refs):
    token_hbm, weight_hbm, out_hbm = refs[:blocks], refs[blocks : blocks + 6], refs[blocks + 6 : 2 * blocks + 6]
    tokens_ref, *weight_refs, out_ref, token_sems, weight_sems, out_sems = refs[2 * blocks + 6 :]
    rows = token_hbm[0].shape[0]
    width = weight_hbm[0].shape[0]
    hidden_units = weight_hbm[0].shape[1]

    token_copies = [
        pltpu.make_async_copy(ref, tokens_ref.at[pl.ds(i * rows, rows)], token_sems.at[i])
        for i, ref in enumerate(token_hbm)
    ]
    weight_copies = [
        pltpu.make_async_copy(source, target, weight_sems.at[i])
        for i, (source, target) in enumerate(zip(weight_hbm, weight_refs))
    ]
    for copy in token_copies + weight_copies:
        copy.start()
    for copy in token_copies:
        copy.wait()

    experts = router_ref.shape[0]
    logits = lax.dot_general(
        tokens_ref[:, :width], router_ref[...], (((1,), (1,)), ((), ())), preferred_element_type=jnp.float32
    )
    named = tokens_ref[:, width:][:, :experts].astype(jnp.float32)
    chosen = named * jax.nn.sigmoid(logits)
    weights = ROUTE_SCALE * chosen / jnp.sum(chosen, axis=1, keepdims=True)
    lanes = lax.broadcasted_iota(jnp.int32, weights.shape, 1)

    def product(i):
        weight_copies[i].wait()
        return jnp.dot(tokens_ref[:, :width], weight_refs[i][...], preferred_element_type=jnp.float32)

    acts, columns = [], []
    for i in range(2):
        gate_part = product(2 * i)
        up_part = product(2 * i + 1)
        acts.append((jax.nn.silu(gate_part) * up_part).astype(jnp.bfloat16))
        columns.append(jnp.sum(jnp.where(lanes == ids_ref[i], weights, 0.0), axis=1, keepdims=True))

    for i in (4, 5):
        weight_copies[i].wait()
    out_copies = []
    for j in range(width // n_tile):
        span = pl.ds(j * n_tile, n_tile)
        total = columns[0] * jnp.dot(
            acts[0], weight_refs[4][:, span], preferred_element_type=jnp.float32
        ) + columns[1] * jnp.dot(acts[1], weight_refs[5][:, span], preferred_element_type=jnp.float32)
        out_ref[:, span] = total.astype(jnp.bfloat16)
        for i, ref in enumerate(out_hbm):
            copy = pltpu.make_async_copy(
                out_ref.at[pl.ds(i * rows, rows), span], ref.at[:, span], out_sems.at[j, i]
            )
            copy.start()
            out_copies.append(copy)
    for copy in out_copies:
        copy.wait()


def experts(ids, token_blocks, router_t, gates, ups, downs):
    blocks = len(token_blocks)
    rows = token_blocks[0].shape[0]
    width, hidden_units = gates[0].shape
    n_tile = 1024
    all_rows = blocks * rows
    weights = (gates[0], ups[0], gates[1], ups[1], downs[0], downs[1])
    return pl.pallas_call(
        functools.partial(experts_kernel, blocks, n_tile),
        in_specs=[pl.BlockSpec(memory_space=pltpu.SMEM), pl.BlockSpec(memory_space=pltpu.VMEM)]
        + [pl.BlockSpec(memory_space=pl.ANY)] * blocks
        + [pl.BlockSpec(memory_space=pl.ANY)] * 6,
        out_specs=[pl.BlockSpec(memory_space=pl.ANY)] * blocks,
        out_shape=[jax.ShapeDtypeStruct((rows, width), jnp.bfloat16)] * blocks,
        scratch_shapes=[pltpu.VMEM((all_rows, width + LANES), jnp.bfloat16)]
        + [pltpu.VMEM(w.shape, jnp.bfloat16) for w in weights]
        + [
            pltpu.VMEM((all_rows, width), jnp.bfloat16),
            pltpu.SemaphoreType.DMA((blocks,)),
            pltpu.SemaphoreType.DMA((6,)),
            pltpu.SemaphoreType.DMA((width // n_tile, blocks)),
        ],
        compiler_params=pltpu.CompilerParams(vmem_limit_bytes=EXPERTS_VMEM),
        cost_estimate=pl.CostEstimate(
            flops=12 * all_rows * width * hidden_units,
            bytes_accessed=12 * width * hidden_units + 4 * all_rows * width,
            transcendentals=2 * all_rows * hidden_units,
        ),
        name="experts",
    )(ids, router_t, *token_blocks, *weights)


def local(hidden, gain, router_w, routes, w_gate, w_up, w_down):
    ep_count, grp_count = lax.axis_size("ep"), lax.axis_size("grp")
    local_experts = ep_count // SPLIT
    expert_count = local_experts * grp_count
    place, core = lax.axis_index("ep") // SPLIT, lax.axis_index("grp")
    plan, return_order, most_open, weights_end, paired = plan_for(ep_count, grp_count)
    rows = hidden.shape[0]
    own = prepare(hidden, gain, routes)
    if paired:
        own = jnp.concatenate([own, between_cores(own)], axis=0)
    weights = [(w[0, 0], between_cores(after(w[0, 0], [own]))) for w in (w_gate, w_up, w_down)]
    held = [own]
    for slot, (parent, *bits) in enumerate(plan, 1):
        ended = held[1 : slot + 1 - most_open[slot - 1]]
        if slot in weights_end:
            ended.append(weights[weights_end[slot]][1])
        held.append(across(after(held[parent], ended), bits, ep_count))
    first = 0
    if paired:
        first = 1
        spare = [0 in bits for _, *bits in plan].index(True) + 1
        held[spare] = jnp.where(core == 1, own, held[spare])

    ids = jnp.stack([core * local_experts + place, (1 - core) * local_experts + place]).astype(jnp.int32)
    router_t = jnp.pad(router_w.T, ((0, -expert_count % 16), (0, 0)))
    parts = experts(ids, held[first:], router_t, *weights)

    terms = [[] for _ in range(first)] + [[part] for part in parts]
    if paired:
        terms[0].append(jnp.where(core == 1, parts[spare - 1], jnp.zeros_like(parts[spare - 1])))

    def summed(slot):
        return sum(term.astype(jnp.float32) for term in terms[slot])

    returned = []
    for slot in return_order:
        parent, *bits = plan[slot - 1]
        value = after(summed(slot).astype(jnp.bfloat16), returned[: max(0, len(returned) + 1 - OPEN_RETURN)])
        returned.append(across(value, bits, ep_count))
        terms[parent].append(returned[-1])
    total = summed(0)
    if paired:
        arrived = between_cores(total[rows:].astype(jnp.bfloat16))
        total = total[:rows] + arrived.astype(jnp.float32)
    return total.astype(jnp.bfloat16)


def solution(mesh):
    in_specs = (
        P(("dom", "ep", "grp"), None),
        P(),
        P(),
        P(("dom", "ep", "grp"), None),
        P("ep", "grp", None, None),
        P("ep", "grp", None, None),
        P("ep", "grp", None, None),
    )
    out_specs = P(("dom", "ep", "grp"), None)
    return jax.shard_map(local, mesh=mesh, in_specs=in_specs, out_specs=out_specs, check_vma=False)
```

```python
import functools

import jax
import jax.numpy as jnp
from jax import lax
from jax.experimental import pallas as pl
from jax.experimental.pallas import tpu as pltpu
from jax.sharding import PartitionSpec as P

SPLIT = 4
LANES = 128

EPSILON = 1e-06
ROUTE_SCALE = 2.5
PREPARE_VMEM = 60 * 1024 * 1024
EXPERTS_VMEM = 44 * 1024 * 1024

PLAN_16 = ((0, 8, 4), (0, 1, 2), (1, 2, 8), (1, 1, 1), (3, 4, 1), (2, 2, 4), (4, 2, 2), (5, 1, 0))
RETURN_16 = tuple((slot, PLAN_16[slot - 1]) for slot in (8, 7, 5, 4, 3, 6, 1, 2))
OPEN_16 = (2, 2, 2, 2, 2, 3, 4, 4)
WEIGHTS_END_16 = {6: 0, 7: 1}
OPEN_RETURN = 5
RETURN_PARTS = 2


def plan_for(ep_count, grp_count):
    if ep_count == 16 and grp_count == 2:
        return PLAN_16, RETURN_16, OPEN_16, WEIGHTS_END_16, True
    plan = []
    for r in range(1, ep_count):
        bit = 1 << (r.bit_length() - 1)
        plan.append((r ^ bit, bit, bit))
    slots = len(plan)
    back = tuple((slot, plan[slot - 1]) for slot in range(slots, 0, -1))
    return tuple(plan), back, (OPEN_RETURN,) * slots, {}, False


def across(value, bits, ep_count):
    pairs = [(i * 2 + c, (i ^ bit) * 2 + c) for c, bit in enumerate(bits) if bit for i in range(ep_count)]
    return lax.ppermute(value, ("ep", "grp"), pairs)


def after(value, earlier):
    return lax.optimization_barrier((value, *earlier))[0] if earlier else value


def between_cores(value):
    return lax.ppermute(value, "grp", [(0, 1), (1, 0)])


def prepare_kernel(count, *refs):
    sources, out_ref, targets, sems = refs[: 2 * count + 1], refs[2 * count + 1], refs[2 * count + 2 : -1], refs[-1]
    copies = [
        pltpu.make_async_copy(source, target, sems.at[i]) for i, (source, target) in enumerate(zip(sources, targets))
    ]
    for copy in copies:
        copy.start()
    for copy in copies:
        copy.wait()
    gain = targets[0][...]
    for i in range(count):
        values = targets[1 + i][...].astype(jnp.float32)
        routes = targets[1 + count + i][...]
        rows, width = values.shape
        span = pl.ds(i * rows, rows)
        square_mean = jnp.mean(values * values, axis=1, keepdims=True)
        normed = values * lax.rsqrt(square_mean + EPSILON) * gain
        out_ref[span, :width] = normed.astype(jnp.bfloat16)
        experts_down = lax.broadcasted_iota(jnp.int32, (LANES, rows), 0)
        named = jnp.zeros((LANES, rows), jnp.float32)
        for k in range(routes.shape[0]):
            named = jnp.where(experts_down == routes[k : k + 1, :], 1.0, named)
        same = lax.broadcasted_iota(jnp.int32, (rows, rows), 0) == lax.broadcasted_iota(jnp.int32, (rows, rows), 1)
        out_ref[span, width:] = lax.dot_general(
            same.astype(jnp.bfloat16),
            named.astype(jnp.bfloat16),
            (((1,), (1,)), ((), ())),
            preferred_element_type=jnp.float32,
        ).astype(jnp.bfloat16)


def prepare(gain, hiddens, routes):
    rows, width = hiddens[0].shape
    count = len(hiddens)
    operands = (gain[None, :], *hiddens, *routes)
    return pl.pallas_call(
        functools.partial(prepare_kernel, count),
        out_shape=jax.ShapeDtypeStruct((count * rows, width + LANES), jnp.bfloat16),
        in_specs=[pl.BlockSpec(memory_space=pl.ANY)] * len(operands),
        scratch_shapes=[pltpu.VMEM(x.shape, x.dtype) for x in operands] + [pltpu.SemaphoreType.DMA((len(operands),))],
        compiler_params=pltpu.CompilerParams(vmem_limit_bytes=PREPARE_VMEM),
        cost_estimate=pl.CostEstimate(
            flops=6 * count * rows * width, bytes_accessed=4 * count * rows * width, transcendentals=count * rows
        ),
        name="prepare",
    )(*operands)


def experts_kernel(blocks, parts, k_steps, n_steps, k_tile, ids_ref, *refs):
    token_refs = refs[:blocks]
    router_ref, gate0_ref, gate1_ref, up0_ref, up1_ref, down0_ref, down1_ref = refs[blocks : blocks + 7]
    out_refs = refs[blocks + 7 : (1 + parts) * blocks + 7]
    gates_ref, logits_ref, act_ref, coeff_ref = refs[(1 + parts) * blocks + 7 :]
    step = pl.program_id(0)
    rows = token_refs[0].shape[0]
    hidden_units = gate0_ref.shape[1]
    width = k_steps * k_tile

    @pl.when(step < k_steps)
    def _():
        columns = pl.ds(pl.multiple_of(step * k_tile, LANES), k_tile)
        tokens = jnp.concatenate([ref[:, columns] for ref in token_refs], axis=0)
        parts = [
            jnp.dot(tokens, ref[...], preferred_element_type=jnp.float32)
            for ref in (gate0_ref, gate1_ref, up0_ref, up1_ref)
        ]
        logits = lax.dot_general(
            tokens, router_ref[...], (((1,), (1,)), ((), ())), preferred_element_type=jnp.float32
        )

        @pl.when(step == 0)
        def _():
            for i, part in enumerate(parts):
                gates_ref[:, i * hidden_units : (i + 1) * hidden_units] = part
            logits_ref[...] = logits

        @pl.when(step > 0)
        def _():
            for i, part in enumerate(parts):
                gates_ref[:, i * hidden_units : (i + 1) * hidden_units] += part
            logits_ref[...] += logits

    @pl.when(step == k_steps - 1)
    def _():
        gate_part = gates_ref[:, : 2 * hidden_units]
        up_part = gates_ref[:, 2 * hidden_units :]
        act_ref[...] = (jax.nn.silu(gate_part) * up_part).astype(jnp.bfloat16)
        named = jnp.concatenate([ref[:, width : width + LANES] for ref in token_refs], axis=0)
        experts = logits_ref.shape[1]
        scores = jax.nn.sigmoid(logits_ref[...])
        chosen = named[:, :experts].astype(jnp.float32) * scores
        weights = ROUTE_SCALE * chosen / jnp.sum(chosen, axis=1, keepdims=True)
        lanes = lax.broadcasted_iota(jnp.int32, weights.shape, 1)
        for i in range(2):
            column = jnp.sum(jnp.where(lanes == ids_ref[i], weights, 0.0), axis=1, keepdims=True)
            coeff_ref[:, i * LANES : (i + 1) * LANES] = jnp.broadcast_to(column, (column.shape[0], LANES))

    @pl.when(step >= k_steps)
    def _():
        total = coeff_ref[:, 0:1] * jnp.dot(
            act_ref[:, :hidden_units], down0_ref[...], preferred_element_type=jnp.float32
        ) + coeff_ref[:, LANES : LANES + 1] * jnp.dot(
            act_ref[:, hidden_units:], down1_ref[...], preferred_element_type=jnp.float32
        )
        part_steps = n_steps // parts
        for part in range(parts):

            @pl.when((step - k_steps) // part_steps == part)
            def _():
                for i, ref in enumerate(out_refs[part * blocks : (part + 1) * blocks]):
                    ref[...] = total[i * rows : (i + 1) * rows].astype(jnp.bfloat16)


def experts(ids, token_blocks, parts, router_t, gates, ups, downs):
    blocks = len(token_blocks)
    rows = token_blocks[0].shape[0]
    width, hidden_units = gates[0].shape
    k_tile = n_tile = width // 4
    k_steps, n_steps = width // k_tile, width // n_tile
    all_rows = blocks * rows

    def at_k(step, ids_ref):
        return jnp.minimum(step, k_steps - 1)

    def at_n(step, ids_ref):
        return jnp.maximum(step - k_steps, 0)

    whole = pl.BlockSpec(token_blocks[0].shape, lambda step, ids_ref: (0, 0))
    in_specs = [whole] * blocks
    in_specs += [pl.BlockSpec((router_t.shape[0], k_tile), lambda step, ids_ref: (0, at_k(step, ids_ref)))]
    in_specs += [pl.BlockSpec((k_tile, hidden_units), lambda step, ids_ref: (at_k(step, ids_ref), 0))] * 4
    in_specs += [pl.BlockSpec((hidden_units, n_tile), lambda step, ids_ref: (0, at_n(step, ids_ref)))] * 2
    part_steps = n_steps // parts

    def at_part(part, step, ids_ref):
        return 0, jnp.clip(step - k_steps - part * part_steps, 0, part_steps - 1)

    out_specs = [
        pl.BlockSpec((rows, n_tile), functools.partial(at_part, part)) for part in range(parts) for _ in range(blocks)
    ]
    return pl.pallas_call(
        functools.partial(experts_kernel, blocks, parts, k_steps, n_steps, k_tile),
        grid_spec=pltpu.PrefetchScalarGridSpec(
            num_scalar_prefetch=1,
            grid=(k_steps + n_steps,),
            in_specs=in_specs,
            out_specs=out_specs,
            scratch_shapes=[
                pltpu.VMEM((all_rows, 4 * hidden_units), jnp.float32),
                pltpu.VMEM((all_rows, router_t.shape[0]), jnp.float32),
                pltpu.VMEM((all_rows, 2 * hidden_units), jnp.bfloat16),
                pltpu.VMEM((all_rows, 2 * LANES), jnp.float32),
            ],
        ),
        out_shape=[jax.ShapeDtypeStruct((rows, width // parts), jnp.bfloat16)] * (blocks * parts),
        compiler_params=pltpu.CompilerParams(vmem_limit_bytes=EXPERTS_VMEM),
        cost_estimate=pl.CostEstimate(
            flops=12 * all_rows * width * hidden_units,
            bytes_accessed=12 * width * hidden_units + 4 * all_rows * width,
            transcendentals=2 * all_rows * hidden_units,
        ),
        name="experts",
    )(ids, *token_blocks, router_t, *gates, *ups, *downs)


def local(hidden, gain, router_w, routes, w_gate, w_up, w_down):
    ep_count, grp_count = lax.axis_size("ep"), lax.axis_size("grp")
    local_experts = ep_count // SPLIT
    expert_count = local_experts * grp_count
    place, core = lax.axis_index("ep") // SPLIT, lax.axis_index("grp")
    plan, return_plan, most_open, weights_end, paired = plan_for(ep_count, grp_count)
    rows = hidden.shape[0]
    hiddens, chosen = [hidden], [routes.T]
    if paired:
        hiddens.append(between_cores(hidden))
        chosen.append(between_cores(routes.T))
    own = prepare(gain, hiddens, chosen)
    weights = [(w[0, 0], between_cores(after(w[0, 0], hiddens[1:] + chosen[1:]))) for w in (w_gate, w_up, w_down)]
    held = [own]
    for slot, (parent, *bits) in enumerate(plan, 1):
        ended = held[1 : slot + 1 - most_open[slot - 1]]
        if slot in weights_end:
            ended.append(weights[weights_end[slot]][1])
        held.append(across(after(held[parent], ended), bits, ep_count))
    first = 0
    if paired:
        first = 1
        spare = [0 in bits for _, *bits in plan].index(True) + 1
        held[spare] = jnp.where(core == 1, own, held[spare])

    ids = jnp.stack([core * local_experts + place, (1 - core) * local_experts + place]).astype(jnp.int32)
    router_t = jnp.pad(router_w.T, ((0, -expert_count % 16), (0, 0)))
    outs = experts(ids, held[first:], RETURN_PARTS, router_t, *weights)
    blocks = len(outs) // RETURN_PARTS

    terms = {}
    for part in range(RETURN_PARTS):
        mine = outs[part * blocks : (part + 1) * blocks]
        terms.update({(part, slot): [value] for slot, value in enumerate(mine, first)})
        if paired:
            terms[part, 0] = [jnp.where(core == 1, mine[spare - 1], jnp.zeros_like(mine[spare - 1]))]

    def summed(part, slot):
        return sum(term.astype(jnp.float32) for term in terms[part, slot])

    returned = []
    for slot, (parent, *bits) in return_plan:
        for part in range(RETURN_PARTS):
            value = summed(part, slot).astype(jnp.bfloat16)
            value = after(value, returned[: max(0, len(returned) + 1 - OPEN_RETURN)])
            returned.append(across(value, bits, ep_count))
            terms[part, parent].append(returned[-1])
    totals = [summed(part, 0) for part in range(RETURN_PARTS)]
    if paired:
        arrived = [between_cores(total[rows:].astype(jnp.bfloat16)) for total in totals]
        totals = [total[:rows] + value.astype(jnp.float32) for total, value in zip(totals, arrived)]
    return jnp.concatenate([total.astype(jnp.bfloat16) for total in totals], axis=1)


def solution(mesh):
    in_specs = (
        P(("dom", "ep", "grp"), None),
        P(),
        P(),
        P(("dom", "ep", "grp"), None),
        P("ep", "grp", None, None),
        P("ep", "grp", None, None),
        P("ep", "grp", None, None),
    )
    out_specs = P(("dom", "ep", "grp"), None)
    return jax.shard_map(local, mesh=mesh, in_specs=in_specs, out_specs=out_specs, check_vma=False)
```

```python
import functools

import jax
import jax.numpy as jnp
from jax import lax
from jax.experimental import pallas as pl
from jax.experimental.pallas import tpu as pltpu
from jax.sharding import PartitionSpec as P

SPLIT = 4
LANES = 128

EPSILON = 1e-06
ROUTE_SCALE = 2.5
PREPARE_VMEM = 60 * 1024 * 1024
EXPERTS_VMEM = 47 * 1024 * 1024

PLAN_16 = ((0, 1, 2), (0, 8, 4), (2, 4, 1), (2, 2, 2), (2, 1, 0), (3, 1, 2), (4, 1, 8), (6, 2, 4))
RETURN_16 = tuple((slot, PLAN_16[slot - 1]) for slot in (8, 7, 6, 4, 5, 3, 2, 1))
OPEN_16 = (2, 2, 2, 2, 2, 3, 4, 4)
WEIGHTS_END_16 = {6: 0, 7: 1}
OPEN_RETURN = 4
EARLY = 5


def plan_for(ep_count, grp_count):
    if ep_count == 16 and grp_count == 2:
        return PLAN_16, RETURN_16, OPEN_16, WEIGHTS_END_16, True
    plan = []
    for r in range(1, ep_count):
        bit = 1 << (r.bit_length() - 1)
        plan.append((r ^ bit, bit, bit))
    slots = len(plan)
    back = tuple((slot, plan[slot - 1]) for slot in range(slots, 0, -1))
    return tuple(plan), back, (OPEN_RETURN,) * slots, {}, False


def across(value, bits, ep_count):
    pairs = [(i * 2 + c, (i ^ bit) * 2 + c) for c, bit in enumerate(bits) if bit for i in range(ep_count)]
    return lax.ppermute(value, ("ep", "grp"), pairs)


def after(value, earlier):
    return lax.optimization_barrier((value, *earlier))[0] if earlier else value


def between_cores(value):
    return lax.ppermute(value, "grp", [(0, 1), (1, 0)])


def prepare_kernel(count, *refs):
    sources, out_ref, targets, sems = refs[: 2 * count + 1], refs[2 * count + 1], refs[2 * count + 2 : -1], refs[-1]
    copies = [
        pltpu.make_async_copy(source, target, sems.at[i]) for i, (source, target) in enumerate(zip(sources, targets))
    ]
    for copy in copies:
        copy.start()
    for copy in copies:
        copy.wait()
    gain = targets[0][...]
    for i in range(count):
        values = targets[1 + i][...].astype(jnp.float32)
        routes = targets[1 + count + i][...]
        rows, width = values.shape
        span = pl.ds(i * rows, rows)
        square_mean = jnp.mean(values * values, axis=1, keepdims=True)
        normed = values * lax.rsqrt(square_mean + EPSILON) * gain
        out_ref[span, :width] = normed.astype(jnp.bfloat16)
        experts_down = lax.broadcasted_iota(jnp.int32, (LANES, rows), 0)
        named = jnp.zeros((LANES, rows), jnp.float32)
        for k in range(routes.shape[0]):
            named = jnp.where(experts_down == routes[k : k + 1, :], 1.0, named)
        same = lax.broadcasted_iota(jnp.int32, (rows, rows), 0) == lax.broadcasted_iota(jnp.int32, (rows, rows), 1)
        out_ref[span, width:] = lax.dot_general(
            same.astype(jnp.bfloat16),
            named.astype(jnp.bfloat16),
            (((1,), (1,)), ((), ())),
            preferred_element_type=jnp.float32,
        ).astype(jnp.bfloat16)


def prepare(gain, hiddens, routes):
    rows, width = hiddens[0].shape
    count = len(hiddens)
    operands = (gain[None, :], *hiddens, *routes)
    return pl.pallas_call(
        functools.partial(prepare_kernel, count),
        out_shape=jax.ShapeDtypeStruct((count * rows, width + LANES), jnp.bfloat16),
        in_specs=[pl.BlockSpec(memory_space=pl.ANY)] * len(operands),
        scratch_shapes=[pltpu.VMEM(x.shape, x.dtype) for x in operands] + [pltpu.SemaphoreType.DMA((len(operands),))],
        compiler_params=pltpu.CompilerParams(vmem_limit_bytes=PREPARE_VMEM),
        cost_estimate=pl.CostEstimate(
            flops=6 * count * rows * width, bytes_accessed=4 * count * rows * width, transcendentals=count * rows
        ),
        name="prepare",
    )(*operands)


def add_products(step, k_tile, token_refs, router_ref, weight_refs, gates_ref, logits_ref):
    hidden_units = weight_refs[0].shape[1]
    columns = pl.ds(pl.multiple_of(step * k_tile, LANES), k_tile)
    tokens = jnp.concatenate([ref[:, columns] for ref in token_refs], axis=0)
    parts = [jnp.dot(tokens, ref[...], preferred_element_type=jnp.float32) for ref in weight_refs]
    logits = lax.dot_general(
        tokens, router_ref[...], (((1,), (1,)), ((), ())), preferred_element_type=jnp.float32
    )

    @pl.when(step == 0)
    def _():
        for i, part in enumerate(parts):
            gates_ref[:, i * hidden_units : (i + 1) * hidden_units] = part
        logits_ref[...] = logits

    @pl.when(step > 0)
    def _():
        for i, part in enumerate(parts):
            gates_ref[:, i * hidden_units : (i + 1) * hidden_units] += part
        logits_ref[...] += logits


def activate(width, ids_ref, token_refs, gates_ref, logits_ref):
    half = gates_ref.shape[1] // 2
    act = (jax.nn.silu(gates_ref[:, :half]) * gates_ref[:, half:]).astype(jnp.bfloat16)
    named = jnp.concatenate([ref[:, width : width + LANES] for ref in token_refs], axis=0)
    chosen = named[:, : logits_ref.shape[1]].astype(jnp.float32) * jax.nn.sigmoid(logits_ref[...])
    weights = ROUTE_SCALE * chosen / jnp.sum(chosen, axis=1, keepdims=True)
    lanes = lax.broadcasted_iota(jnp.int32, weights.shape, 1)
    columns = []
    for i in range(2):
        column = jnp.sum(jnp.where(lanes == ids_ref[i], weights, 0.0), axis=1, keepdims=True)
        columns.append(jnp.broadcast_to(column, (column.shape[0], LANES)))
    return act, jnp.concatenate(columns, axis=1)


def early_kernel(blocks, k_steps, k_tile, ids_ref, *refs):
    token_refs, router_ref, weight_refs = refs[:blocks], refs[blocks], refs[blocks + 1 : blocks + 5]
    act_ref, coeff_ref, gates_ref, logits_ref = refs[blocks + 5 :]
    step = pl.program_id(0)
    add_products(step, k_tile, token_refs, router_ref, weight_refs, gates_ref, logits_ref)

    @pl.when(step == k_steps - 1)
    def _():
        act_ref[...], coeff_ref[...] = activate(k_steps * k_tile, ids_ref, token_refs, gates_ref, logits_ref)


def early(ids, token_blocks, router_t, gates, ups):
    blocks = len(token_blocks)
    width, hidden_units = gates[0].shape
    rows = blocks * token_blocks[0].shape[0]
    k_steps = 4
    k_tile = width // k_steps
    return pl.pallas_call(
        functools.partial(early_kernel, blocks, k_steps, k_tile),
        grid_spec=pltpu.PrefetchScalarGridSpec(
            num_scalar_prefetch=1,
            grid=(k_steps,),
            in_specs=[pl.BlockSpec(token_blocks[0].shape, lambda step, ids_ref: (0, 0))] * blocks
            + [pl.BlockSpec((router_t.shape[0], k_tile), lambda step, ids_ref: (0, step))]
            + [pl.BlockSpec((k_tile, hidden_units), lambda step, ids_ref: (step, 0))] * 4,
            out_specs=[
                pl.BlockSpec((rows, 2 * hidden_units), lambda step, ids_ref: (0, 0)),
                pl.BlockSpec((rows, 2 * LANES), lambda step, ids_ref: (0, 0)),
            ],
            scratch_shapes=[
                pltpu.VMEM((rows, 4 * hidden_units), jnp.float32),
                pltpu.VMEM((rows, router_t.shape[0]), jnp.float32),
            ],
        ),
        out_shape=[
            jax.ShapeDtypeStruct((rows, 2 * hidden_units), jnp.bfloat16),
            jax.ShapeDtypeStruct((rows, 2 * LANES), jnp.float32),
        ],
        compiler_params=pltpu.CompilerParams(vmem_limit_bytes=EXPERTS_VMEM),
        cost_estimate=pl.CostEstimate(
            flops=8 * rows * width * hidden_units,
            bytes_accessed=8 * width * hidden_units + 2 * rows * width,
            transcendentals=2 * rows * hidden_units,
        ),
        name="early",
    )(ids, *token_blocks, router_t, *gates, *ups)


def experts_kernel(blocks, done_rows, rows, k_steps, k_tile, ids_ref, *refs):
    token_refs, router_ref = refs[:blocks], refs[blocks]
    weight_refs, down0_ref, down1_ref = refs[blocks + 1 : blocks + 5], refs[blocks + 5], refs[blocks + 6]
    refs = refs[blocks + 7 :]
    if done_rows:
        done_act_ref, done_coeff_ref, *refs = refs
    *out_refs, gates_ref, logits_ref, act_ref, coeff_ref = refs
    hidden_units = weight_refs[0].shape[1]
    step = pl.program_id(0)

    @pl.when(step < k_steps)
    def _():
        add_products(step, k_tile, token_refs, router_ref, weight_refs, gates_ref, logits_ref)

    @pl.when(step == k_steps - 1)
    def _():
        act, coeff = activate(k_steps * k_tile, ids_ref, token_refs, gates_ref, logits_ref)
        act_ref[done_rows:, :] = act
        coeff_ref[done_rows:, :] = coeff
        if done_rows:
            act_ref[:done_rows, :] = done_act_ref[...]
            coeff_ref[:done_rows, :] = done_coeff_ref[...]

    @pl.when(step >= k_steps)
    def _():
        total = coeff_ref[:, 0:1] * jnp.dot(
            act_ref[:, :hidden_units], down0_ref[...], preferred_element_type=jnp.float32
        ) + coeff_ref[:, LANES : LANES + 1] * jnp.dot(
            act_ref[:, hidden_units:], down1_ref[...], preferred_element_type=jnp.float32
        )
        for i, ref in enumerate(out_refs):
            ref[...] = total[i * rows : (i + 1) * rows].astype(jnp.bfloat16)


def experts(ids, token_blocks, done, router_t, gates, ups, downs):
    blocks = len(token_blocks)
    rows = token_blocks[0].shape[0]
    width, hidden_units = gates[0].shape
    k_steps = n_steps = 4
    k_tile, n_tile = width // k_steps, width // n_steps
    late_rows = blocks * rows
    done_rows = done[0].shape[0] if done else 0
    all_rows = done_rows + late_rows
    outs = all_rows // rows

    def at_k(step):
        return jnp.minimum(step, k_steps - 1)

    def at_n(step):
        return jnp.maximum(step - k_steps, 0)

    in_specs = [pl.BlockSpec(token_blocks[0].shape, lambda step, ids_ref: (0, 0))] * blocks
    in_specs += [pl.BlockSpec((router_t.shape[0], k_tile), lambda step, ids_ref: (0, at_k(step)))]
    in_specs += [pl.BlockSpec((k_tile, hidden_units), lambda step, ids_ref: (at_k(step), 0))] * 4
    in_specs += [pl.BlockSpec((hidden_units, n_tile), lambda step, ids_ref: (0, at_n(step)))] * 2
    in_specs += [pl.BlockSpec(x.shape, lambda step, ids_ref: (0, 0)) for x in done]
    return pl.pallas_call(
        functools.partial(experts_kernel, blocks, done_rows, rows, k_steps, k_tile),
        grid_spec=pltpu.PrefetchScalarGridSpec(
            num_scalar_prefetch=1,
            grid=(k_steps + n_steps,),
            in_specs=in_specs,
            out_specs=[pl.BlockSpec((rows, n_tile), lambda step, ids_ref: (0, at_n(step)))] * outs,
            scratch_shapes=[
                pltpu.VMEM((late_rows, 4 * hidden_units), jnp.float32),
                pltpu.VMEM((late_rows, router_t.shape[0]), jnp.float32),
                pltpu.VMEM((all_rows, 2 * hidden_units), jnp.bfloat16),
                pltpu.VMEM((all_rows, 2 * LANES), jnp.float32),
            ],
        ),
        out_shape=[jax.ShapeDtypeStruct((rows, width), jnp.bfloat16)] * outs,
        compiler_params=pltpu.CompilerParams(vmem_limit_bytes=EXPERTS_VMEM),
        cost_estimate=pl.CostEstimate(
            flops=(8 * late_rows + 4 * all_rows) * width * hidden_units,
            bytes_accessed=12 * width * hidden_units + 4 * all_rows * width,
            transcendentals=2 * late_rows * hidden_units,
        ),
        name="experts",
    )(ids, *token_blocks, router_t, *gates, *ups, *downs, *done)


def local(hidden, gain, router_w, routes, w_gate, w_up, w_down):
    ep_count, grp_count = lax.axis_size("ep"), lax.axis_size("grp")
    local_experts = ep_count // SPLIT
    expert_count = local_experts * grp_count
    place, core = lax.axis_index("ep") // SPLIT, lax.axis_index("grp")
    plan, return_plan, most_open, weights_end, paired = plan_for(ep_count, grp_count)
    rows = hidden.shape[0]
    hiddens, chosen = [hidden], [routes.T]
    if paired:
        hiddens.append(between_cores(hidden))
        chosen.append(between_cores(routes.T))
    own = prepare(gain, hiddens, chosen)
    weights = [(w[0, 0], between_cores(after(w[0, 0], hiddens[1:] + chosen[1:]))) for w in (w_gate, w_up, w_down)]
    held = [own]
    for slot, (parent, *bits) in enumerate(plan, 1):
        ended = held[1 : slot + 1 - most_open[slot - 1]]
        if slot in weights_end:
            ended.append(weights[weights_end[slot]][1])
        held.append(across(after(held[parent], ended), bits, ep_count))
    first = 0
    if paired:
        first = 1
        spare = [0 in bits for _, *bits in plan].index(True) + 1
        held[spare] = jnp.where(core == 1, own, held[spare])

    ids = jnp.stack([core * local_experts + place, (1 - core) * local_experts + place]).astype(jnp.int32)
    router_t = jnp.pad(router_w.T, ((0, -expert_count % 16), (0, 0)))
    done = early(ids, held[1 : 1 + EARLY], router_t, *weights[:2]) if paired else ()
    outs = experts(ids, held[1 + EARLY :] if paired else held, done, router_t, *weights)

    terms = {slot: [value] for slot, value in enumerate(outs, first)}
    if paired:
        terms[0] = [jnp.where(core == 1, outs[spare - 1], jnp.zeros_like(outs[spare - 1]))]

    def summed(slot):
        return sum(term.astype(jnp.float32) for term in terms[slot])

    returned = []
    for slot, (parent, *bits) in return_plan:
        value = summed(slot).astype(jnp.bfloat16)
        value = after(value, returned[: max(0, len(returned) + 1 - OPEN_RETURN)])
        returned.append(across(value, bits, ep_count))
        terms[parent].append(returned[-1])
    total = summed(0)
    if paired:
        arrived = between_cores(total[rows:].astype(jnp.bfloat16))
        total = total[:rows] + arrived.astype(jnp.float32)
    return total.astype(jnp.bfloat16)


def solution(mesh):
    in_specs = (
        P(("dom", "ep", "grp"), None),
        P(),
        P(),
        P(("dom", "ep", "grp"), None),
        P("ep", "grp", None, None),
        P("ep", "grp", None, None),
        P("ep", "grp", None, None),
    )
    out_specs = P(("dom", "ep", "grp"), None)
    return jax.shard_map(local, mesh=mesh, in_specs=in_specs, out_specs=out_specs, check_vma=False)
```

```python
import functools

import jax
import jax.numpy as jnp
from jax import lax
from jax.experimental import pallas as pl
from jax.experimental.pallas import tpu as pltpu
from jax.sharding import PartitionSpec as P

SPLIT = 4
LANES = 128

EPSILON = 1e-06
ROUTE_SCALE = 2.5
PREPARE_VMEM = 60 * 1024 * 1024
EXPERTS_VMEM = 16 * 1024 * 1024

PLAN_16 = ((0, 1, 2), (0, 8, 4), (2, 4, 1), (2, 2, 2), (2, 1, 0), (3, 1, 2), (4, 1, 8), (6, 2, 4))
RETURN_16 = tuple((slot, PLAN_16[slot - 1]) for slot in (8, 7, 6, 4, 5, 3, 2, 1))
OPEN_16 = (2, 2, 2, 2, 2, 3, 4, 4)
WEIGHTS_END_16 = {6: 0, 7: 1}
OPEN_RETURN = 4
EARLY = 5


def plan_for(ep_count, grp_count):
    if ep_count == 16 and grp_count == 2:
        return PLAN_16, RETURN_16, OPEN_16, WEIGHTS_END_16, True
    plan = []
    for r in range(1, ep_count):
        bit = 1 << (r.bit_length() - 1)
        plan.append((r ^ bit, bit, bit))
    slots = len(plan)
    back = tuple((slot, plan[slot - 1]) for slot in range(slots, 0, -1))
    return tuple(plan), back, (OPEN_RETURN,) * slots, {}, False


def across(value, bits, ep_count):
    pairs = [(i * 2 + c, (i ^ bit) * 2 + c) for c, bit in enumerate(bits) if bit for i in range(ep_count)]
    return lax.ppermute(value, ("ep", "grp"), pairs)


def after(value, earlier):
    return lax.optimization_barrier((value, *earlier))[0] if earlier else value


def between_cores(value):
    return lax.ppermute(value, "grp", [(0, 1), (1, 0)])


def prepare_kernel(count, *refs):
    sources, out_ref, targets, sems = refs[: 2 * count + 1], refs[2 * count + 1], refs[2 * count + 2 : -1], refs[-1]
    copies = [
        pltpu.make_async_copy(source, target, sems.at[i]) for i, (source, target) in enumerate(zip(sources, targets))
    ]
    for copy in copies:
        copy.start()
    for copy in copies:
        copy.wait()
    gain = targets[0][...]
    for i in range(count):
        values = targets[1 + i][...].astype(jnp.float32)
        routes = targets[1 + count + i][...]
        rows, width = values.shape
        span = pl.ds(i * rows, rows)
        square_mean = jnp.mean(values * values, axis=1, keepdims=True)
        normed = values * lax.rsqrt(square_mean + EPSILON) * gain
        out_ref[span, :width] = normed.astype(jnp.bfloat16)
        experts_down = lax.broadcasted_iota(jnp.int32, (LANES, rows), 0)
        named = jnp.zeros((LANES, rows), jnp.float32)
        for k in range(routes.shape[0]):
            named = jnp.where(experts_down == routes[k : k + 1, :], 1.0, named)
        same = lax.broadcasted_iota(jnp.int32, (rows, rows), 0) == lax.broadcasted_iota(jnp.int32, (rows, rows), 1)
        out_ref[span, width:] = lax.dot_general(
            same.astype(jnp.bfloat16),
            named.astype(jnp.bfloat16),
            (((1,), (1,)), ((), ())),
            preferred_element_type=jnp.float32,
        ).astype(jnp.bfloat16)


def prepare(gain, hiddens, routes):
    rows, width = hiddens[0].shape
    count = len(hiddens)
    operands = (gain[None, :], *hiddens, *routes)
    return pl.pallas_call(
        functools.partial(prepare_kernel, count),
        out_shape=jax.ShapeDtypeStruct((count * rows, width + LANES), jnp.bfloat16),
        in_specs=[pl.BlockSpec(memory_space=pl.ANY)] * len(operands),
        scratch_shapes=[pltpu.VMEM(x.shape, x.dtype) for x in operands] + [pltpu.SemaphoreType.DMA((len(operands),))],
        compiler_params=pltpu.CompilerParams(vmem_limit_bytes=PREPARE_VMEM),
        cost_estimate=pl.CostEstimate(
            flops=6 * count * rows * width, bytes_accessed=4 * count * rows * width, transcendentals=count * rows
        ),
        name="prepare",
    )(*operands)


def gate_up(ids_ref, token_refs, router_ref, weight_refs, tokens_ref):
    rows = token_refs[0].shape[0]
    width = weight_refs[0].shape[0]
    for i, ref in enumerate(token_refs):
        tokens_ref[i * rows : (i + 1) * rows, :] = ref[...]

    def product(ref):
        return jnp.dot(tokens_ref[:, :width], ref[...], preferred_element_type=jnp.float32)

    logits = lax.dot_general(
        tokens_ref[:, :width], router_ref[...], (((1,), (1,)), ((), ())), preferred_element_type=jnp.float32
    )
    named = tokens_ref[:, width:][:, : logits.shape[1]].astype(jnp.float32)
    chosen = named * jax.nn.sigmoid(logits)
    weights = ROUTE_SCALE * chosen / jnp.sum(chosen, axis=1, keepdims=True)
    lanes = lax.broadcasted_iota(jnp.int32, weights.shape, 1)
    acts, columns = [], []
    for i in range(2):
        acts.append((jax.nn.silu(product(weight_refs[i])) * product(weight_refs[2 + i])).astype(jnp.bfloat16))
        column = jnp.sum(jnp.where(lanes == ids_ref[i], weights, 0.0), axis=1, keepdims=True)
        columns.append(jnp.broadcast_to(column, (column.shape[0], LANES)))
    return jnp.concatenate(acts, axis=1), jnp.concatenate(columns, axis=1)


def early_kernel(blocks, ids_ref, *refs):
    token_refs, router_ref, weight_refs = refs[:blocks], refs[blocks], refs[blocks + 1 : blocks + 5]
    act_ref, coeff_ref, tokens_ref = refs[blocks + 5 :]
    act_ref[...], coeff_ref[...] = gate_up(ids_ref, token_refs, router_ref, weight_refs, tokens_ref)


def early(ids, token_blocks, router_t, gates, ups):
    blocks = len(token_blocks)
    width, hidden_units = gates[0].shape
    rows = blocks * token_blocks[0].shape[0]
    in_vmem = pl.BlockSpec(memory_space=pltpu.VMEM)
    return pl.pallas_call(
        functools.partial(early_kernel, blocks),
        in_specs=[pl.BlockSpec(memory_space=pltpu.SMEM)] + [in_vmem] * (blocks + 5),
        out_specs=[in_vmem] * 2,
        out_shape=[
            jax.ShapeDtypeStruct((rows, 2 * hidden_units), jnp.bfloat16),
            jax.ShapeDtypeStruct((rows, 2 * LANES), jnp.float32),
        ],
        scratch_shapes=[pltpu.VMEM((rows, width + LANES), jnp.bfloat16)],
        compiler_params=pltpu.CompilerParams(vmem_limit_bytes=EXPERTS_VMEM),
        cost_estimate=pl.CostEstimate(
            flops=8 * rows * width * hidden_units,
            bytes_accessed=8 * width * hidden_units + 2 * rows * width,
            transcendentals=2 * rows * hidden_units,
        ),
        name="early",
    )(ids, *token_blocks, router_t, *gates, *ups)


def experts_kernel(blocks, done_rows, rows, n_tile, ids_ref, *refs):
    token_refs, router_ref = refs[:blocks], refs[blocks]
    weight_refs, down0_ref, down1_ref = refs[blocks + 1 : blocks + 5], refs[blocks + 5], refs[blocks + 6]
    refs = refs[blocks + 7 :]
    if done_rows:
        done_act_ref, done_coeff_ref, *refs = refs
    *out_refs, tokens_ref, act_ref, coeff_ref = refs
    hidden_units, width = down0_ref.shape
    act, coeff = gate_up(ids_ref, token_refs, router_ref, weight_refs, tokens_ref)
    act_ref[done_rows:, :] = act
    coeff_ref[done_rows:, :] = coeff
    if done_rows:
        act_ref[:done_rows, :] = done_act_ref[...]
        coeff_ref[:done_rows, :] = done_coeff_ref[...]
    for j in range(width // n_tile):
        span = slice(j * n_tile, (j + 1) * n_tile)
        total = coeff_ref[:, 0:1] * jnp.dot(
            act_ref[:, :hidden_units], down0_ref[:, span], preferred_element_type=jnp.float32
        ) + coeff_ref[:, LANES : LANES + 1] * jnp.dot(
            act_ref[:, hidden_units:], down1_ref[:, span], preferred_element_type=jnp.float32
        )
        for i, ref in enumerate(out_refs):
            ref[:, span] = total[i * rows : (i + 1) * rows].astype(jnp.bfloat16)


def experts(ids, token_blocks, done, router_t, gates, ups, downs):
    blocks = len(token_blocks)
    rows = token_blocks[0].shape[0]
    width, hidden_units = gates[0].shape
    late_rows = blocks * rows
    done_rows = done[0].shape[0] if done else 0
    all_rows = done_rows + late_rows
    outs = all_rows // rows
    in_vmem = pl.BlockSpec(memory_space=pltpu.VMEM)
    return pl.pallas_call(
        functools.partial(experts_kernel, blocks, done_rows, rows, 1024),
        in_specs=[pl.BlockSpec(memory_space=pltpu.SMEM)] + [in_vmem] * (blocks + 7 + len(done)),
        out_specs=[in_vmem] * outs,
        out_shape=[jax.ShapeDtypeStruct((rows, width), jnp.bfloat16)] * outs,
        scratch_shapes=[
            pltpu.VMEM((late_rows, width + LANES), jnp.bfloat16),
            pltpu.VMEM((all_rows, 2 * hidden_units), jnp.bfloat16),
            pltpu.VMEM((all_rows, 2 * LANES), jnp.float32),
        ],
        compiler_params=pltpu.CompilerParams(vmem_limit_bytes=EXPERTS_VMEM),
        cost_estimate=pl.CostEstimate(
            flops=(8 * late_rows + 4 * all_rows) * width * hidden_units,
            bytes_accessed=12 * width * hidden_units + 4 * all_rows * width,
            transcendentals=2 * late_rows * hidden_units,
        ),
        name="experts",
    )(ids, *token_blocks, router_t, *gates, *ups, *downs, *done)


def local(hidden, gain, router_w, routes, w_gate, w_up, w_down):
    ep_count, grp_count = lax.axis_size("ep"), lax.axis_size("grp")
    local_experts = ep_count // SPLIT
    expert_count = local_experts * grp_count
    place, core = lax.axis_index("ep") // SPLIT, lax.axis_index("grp")
    plan, return_plan, most_open, weights_end, paired = plan_for(ep_count, grp_count)
    rows = hidden.shape[0]
    hiddens, chosen = [hidden], [routes.T]
    if paired:
        hiddens.append(between_cores(hidden))
        chosen.append(between_cores(routes.T))
    own = prepare(gain, hiddens, chosen)
    weights = [(w[0, 0], between_cores(after(w[0, 0], hiddens[1:] + chosen[1:]))) for w in (w_gate, w_up, w_down)]
    held = [own]
    for slot, (parent, *bits) in enumerate(plan, 1):
        ended = held[1 : slot + 1 - most_open[slot - 1]]
        if slot in weights_end:
            ended.append(weights[weights_end[slot]][1])
        held.append(across(after(held[parent], ended), bits, ep_count))
    first = 0
    if paired:
        first = 1
        spare = [0 in bits for _, *bits in plan].index(True) + 1
        held[spare] = jnp.where(core == 1, own, held[spare])

    ids = jnp.stack([core * local_experts + place, (1 - core) * local_experts + place]).astype(jnp.int32)
    router_t = jnp.pad(router_w.T, ((0, -expert_count % 16), (0, 0)))
    done = early(ids, held[1 : 1 + EARLY], router_t, *weights[:2]) if paired else ()
    outs = experts(ids, held[1 + EARLY :] if paired else held, done, router_t, *weights)

    terms = {slot: [value] for slot, value in enumerate(outs, first)}
    if paired:
        terms[0] = [jnp.where(core == 1, outs[spare - 1], jnp.zeros_like(outs[spare - 1]))]

    def summed(slot):
        return sum(term.astype(jnp.float32) for term in terms[slot])

    returned = []
    for slot, (parent, *bits) in return_plan:
        value = summed(slot).astype(jnp.bfloat16)
        value = after(value, returned[: max(0, len(returned) + 1 - OPEN_RETURN)])
        returned.append(across(value, bits, ep_count))
        terms[parent].append(returned[-1])
    total = summed(0)
    if paired:
        arrived = between_cores(total[rows:].astype(jnp.bfloat16))
        total = total[:rows] + arrived.astype(jnp.float32)
    return total.astype(jnp.bfloat16)


def solution(mesh):
    in_specs = (
        P(("dom", "ep", "grp"), None),
        P(),
        P(),
        P(("dom", "ep", "grp"), None),
        P("ep", "grp", None, None),
        P("ep", "grp", None, None),
        P("ep", "grp", None, None),
    )
    out_specs = P(("dom", "ep", "grp"), None)
    return jax.shard_map(local, mesh=mesh, in_specs=in_specs, out_specs=out_specs, check_vma=False)
```

```python
import functools

import jax
import jax.numpy as jnp
from jax import lax
from jax.experimental import pallas as pl
from jax.experimental.pallas import tpu as pltpu
from jax.sharding import PartitionSpec as P

SPLIT = 4
LANES = 128

EPSILON = 1e-06
ROUTE_SCALE = 2.5
PREPARE_VMEM = 60 * 1024 * 1024
EXPERTS_VMEM = 16 * 1024 * 1024
EARLY_VMEM = 36 * 1024 * 1024

PLAN_16 = ((0, 1, 2), (0, 8, 4), (2, 4, 1), (2, 2, 2), (2, 1, 0), (3, 1, 2), (4, 1, 8), (6, 2, 4))
RETURN_16 = tuple((slot, PLAN_16[slot - 1]) for slot in (8, 7, 6, 4, 5, 3, 2, 1))
OPEN_16 = (2, 2, 2, 2, 2, 3, 4, 4)
WEIGHTS_END_16 = {6: 0, 7: 1}
OPEN_RETURN = 4
EARLY = 5


def plan_for(ep_count, grp_count):
    if ep_count == 16 and grp_count == 2:
        return PLAN_16, RETURN_16, OPEN_16, WEIGHTS_END_16, True
    plan = []
    for r in range(1, ep_count):
        bit = 1 << (r.bit_length() - 1)
        plan.append((r ^ bit, bit, bit))
    slots = len(plan)
    back = tuple((slot, plan[slot - 1]) for slot in range(slots, 0, -1))
    return tuple(plan), back, (OPEN_RETURN,) * slots, {}, False


def across(value, bits, ep_count):
    pairs = [(i * 2 + c, (i ^ bit) * 2 + c) for c, bit in enumerate(bits) if bit for i in range(ep_count)]
    return lax.ppermute(value, ("ep", "grp"), pairs)


def after(value, earlier):
    return lax.optimization_barrier((value, *earlier))[0] if earlier else value


def between_cores(value):
    return lax.ppermute(value, "grp", [(0, 1), (1, 0)])


def prepare_kernel(count, *refs):
    sources, out_ref, targets, sems = refs[: 2 * count + 1], refs[2 * count + 1], refs[2 * count + 2 : -1], refs[-1]
    copies = [
        pltpu.make_async_copy(source, target, sems.at[i]) for i, (source, target) in enumerate(zip(sources, targets))
    ]
    for copy in copies:
        copy.start()
    for copy in copies:
        copy.wait()
    gain = targets[0][...]
    for i in range(count):
        values = targets[1 + i][...].astype(jnp.float32)
        routes = targets[1 + count + i][...]
        rows, width = values.shape
        span = pl.ds(i * rows, rows)
        square_mean = jnp.mean(values * values, axis=1, keepdims=True)
        normed = values * lax.rsqrt(square_mean + EPSILON) * gain
        out_ref[span, :width] = normed.astype(jnp.bfloat16)
        experts_down = lax.broadcasted_iota(jnp.int32, (LANES, rows), 0)
        named = jnp.zeros((LANES, rows), jnp.float32)
        for k in range(routes.shape[0]):
            named = jnp.where(experts_down == routes[k : k + 1, :], 1.0, named)
        same = lax.broadcasted_iota(jnp.int32, (rows, rows), 0) == lax.broadcasted_iota(jnp.int32, (rows, rows), 1)
        out_ref[span, width:] = lax.dot_general(
            same.astype(jnp.bfloat16),
            named.astype(jnp.bfloat16),
            (((1,), (1,)), ((), ())),
            preferred_element_type=jnp.float32,
        ).astype(jnp.bfloat16)


def prepare(gain, hiddens, routes):
    rows, width = hiddens[0].shape
    count = len(hiddens)
    operands = (gain[None, :], *hiddens, *routes)
    return pl.pallas_call(
        functools.partial(prepare_kernel, count),
        out_shape=jax.ShapeDtypeStruct((count * rows, width + LANES), jnp.bfloat16),
        in_specs=[pl.BlockSpec(memory_space=pl.ANY)] * len(operands),
        scratch_shapes=[pltpu.VMEM(x.shape, x.dtype) for x in operands] + [pltpu.SemaphoreType.DMA((len(operands),))],
        compiler_params=pltpu.CompilerParams(vmem_limit_bytes=PREPARE_VMEM),
        cost_estimate=pl.CostEstimate(
            flops=6 * count * rows * width, bytes_accessed=4 * count * rows * width, transcendentals=count * rows
        ),
        name="prepare",
    )(*operands)


def gate_up(ids_ref, token_refs, router_ref, weight_refs, tokens_ref, copies=()):
    rows = token_refs[0].shape[0]
    width = weight_refs[0].shape[0]
    for i, ref in enumerate(token_refs):
        tokens_ref[i * rows : (i + 1) * rows, :] = ref[...]

    def product(ref):
        return jnp.dot(tokens_ref[:, :width], ref[...], preferred_element_type=jnp.float32)

    logits = lax.dot_general(
        tokens_ref[:, :width], router_ref[...], (((1,), (1,)), ((), ())), preferred_element_type=jnp.float32
    )
    named = tokens_ref[:, width:][:, : logits.shape[1]].astype(jnp.float32)
    chosen = named * jax.nn.sigmoid(logits)
    weights = ROUTE_SCALE * chosen / jnp.sum(chosen, axis=1, keepdims=True)
    lanes = lax.broadcasted_iota(jnp.int32, weights.shape, 1)
    acts, columns = [None, None], []
    for i in (1, 0):
        if i == 0:
            for copy in copies:
                copy.wait()
        acts[i] = (jax.nn.silu(product(weight_refs[i])) * product(weight_refs[2 + i])).astype(jnp.bfloat16)
    for i in range(2):
        column = jnp.sum(jnp.where(lanes == ids_ref[i], weights, 0.0), axis=1, keepdims=True)
        columns.append(jnp.broadcast_to(column, (column.shape[0], LANES)))
    return jnp.concatenate(acts, axis=1), jnp.concatenate(columns, axis=1)


def early_kernel(blocks, ids_ref, *refs):
    token_refs, router_ref = refs[:blocks], refs[blocks]
    gate1_ref, up1_ref, *own_hbm = refs[blocks + 1 : blocks + 6]
    act_ref, coeff_ref, *own_refs, tokens_ref, sems = refs[blocks + 6 :]
    copies = [
        pltpu.make_async_copy(source, target, sems.at[i]) for i, (source, target) in enumerate(zip(own_hbm, own_refs))
    ]
    for copy in copies:
        copy.start()
    weight_refs = (own_refs[0], gate1_ref, own_refs[1], up1_ref)
    act_ref[...], coeff_ref[...] = gate_up(ids_ref, token_refs, router_ref, weight_refs, tokens_ref, copies[:2])
    copies[2].wait()


def early(ids, token_blocks, router_t, gates, ups, downs):
    blocks = len(token_blocks)
    width, hidden_units = gates[0].shape
    rows = blocks * token_blocks[0].shape[0]
    in_vmem = pl.BlockSpec(memory_space=pltpu.VMEM)
    own = (gates[0], ups[0], downs[0])
    return pl.pallas_call(
        functools.partial(early_kernel, blocks),
        in_specs=[pl.BlockSpec(memory_space=pltpu.SMEM)]
        + [in_vmem] * (blocks + 3)
        + [pl.BlockSpec(memory_space=pl.ANY)] * 3,
        out_specs=[in_vmem] * 5,
        out_shape=[
            jax.ShapeDtypeStruct((rows, 2 * hidden_units), jnp.bfloat16),
            jax.ShapeDtypeStruct((rows, 2 * LANES), jnp.float32),
        ]
        + [jax.ShapeDtypeStruct(w.shape, w.dtype) for w in own],
        scratch_shapes=[pltpu.VMEM((rows, width + LANES), jnp.bfloat16), pltpu.SemaphoreType.DMA((3,))],
        compiler_params=pltpu.CompilerParams(vmem_limit_bytes=EARLY_VMEM),
        cost_estimate=pl.CostEstimate(
            flops=8 * rows * width * hidden_units,
            bytes_accessed=8 * width * hidden_units + 2 * rows * width,
            transcendentals=2 * rows * hidden_units,
        ),
        name="early",
    )(ids, *token_blocks, router_t, gates[1], ups[1], *own)


def experts_kernel(blocks, done_rows, rows, n_tile, ids_ref, *refs):
    token_refs, router_ref = refs[:blocks], refs[blocks]
    weight_refs, down0_ref, down1_ref = refs[blocks + 1 : blocks + 5], refs[blocks + 5], refs[blocks + 6]
    refs = refs[blocks + 7 :]
    if done_rows:
        done_act_ref, done_coeff_ref, *refs = refs
    *out_refs, tokens_ref, act_ref, coeff_ref = refs
    hidden_units, width = down0_ref.shape
    act, coeff = gate_up(ids_ref, token_refs, router_ref, weight_refs, tokens_ref)
    act_ref[done_rows:, :] = act
    coeff_ref[done_rows:, :] = coeff
    if done_rows:
        act_ref[:done_rows, :] = done_act_ref[...]
        coeff_ref[:done_rows, :] = done_coeff_ref[...]
    for j in range(width // n_tile):
        span = slice(j * n_tile, (j + 1) * n_tile)
        total = coeff_ref[:, 0:1] * jnp.dot(
            act_ref[:, :hidden_units], down0_ref[:, span], preferred_element_type=jnp.float32
        ) + coeff_ref[:, LANES : LANES + 1] * jnp.dot(
            act_ref[:, hidden_units:], down1_ref[:, span], preferred_element_type=jnp.float32
        )
        for i, ref in enumerate(out_refs):
            ref[:, span] = total[i * rows : (i + 1) * rows].astype(jnp.bfloat16)


def experts(ids, token_blocks, done, router_t, gates, ups, downs):
    blocks = len(token_blocks)
    rows = token_blocks[0].shape[0]
    width, hidden_units = gates[0].shape
    late_rows = blocks * rows
    done_rows = done[0].shape[0] if done else 0
    all_rows = done_rows + late_rows
    outs = all_rows // rows
    in_vmem = pl.BlockSpec(memory_space=pltpu.VMEM)
    return pl.pallas_call(
        functools.partial(experts_kernel, blocks, done_rows, rows, 1024),
        in_specs=[pl.BlockSpec(memory_space=pltpu.SMEM)] + [in_vmem] * (blocks + 7 + len(done)),
        out_specs=[in_vmem] * outs,
        out_shape=[jax.ShapeDtypeStruct((rows, width), jnp.bfloat16)] * outs,
        scratch_shapes=[
            pltpu.VMEM((late_rows, width + LANES), jnp.bfloat16),
            pltpu.VMEM((all_rows, 2 * hidden_units), jnp.bfloat16),
            pltpu.VMEM((all_rows, 2 * LANES), jnp.float32),
        ],
        compiler_params=pltpu.CompilerParams(vmem_limit_bytes=EXPERTS_VMEM),
        cost_estimate=pl.CostEstimate(
            flops=(8 * late_rows + 4 * all_rows) * width * hidden_units,
            bytes_accessed=12 * width * hidden_units + 4 * all_rows * width,
            transcendentals=2 * late_rows * hidden_units,
        ),
        name="experts",
    )(ids, *token_blocks, router_t, *gates, *ups, *downs, *done)


def local(hidden, gain, router_w, routes, w_gate, w_up, w_down):
    ep_count, grp_count = lax.axis_size("ep"), lax.axis_size("grp")
    local_experts = ep_count // SPLIT
    expert_count = local_experts * grp_count
    place, core = lax.axis_index("ep") // SPLIT, lax.axis_index("grp")
    plan, return_plan, most_open, weights_end, paired = plan_for(ep_count, grp_count)
    rows = hidden.shape[0]
    hiddens, chosen = [hidden], [routes.T]
    if paired:
        hiddens.append(between_cores(hidden))
        chosen.append(between_cores(routes.T))
    own = prepare(gain, hiddens, chosen)
    weights = [(w[0, 0], between_cores(after(w[0, 0], hiddens[1:] + chosen[1:]))) for w in (w_gate, w_up, w_down)]
    held = [own]
    for slot, (parent, *bits) in enumerate(plan, 1):
        ended = held[1 : slot + 1 - most_open[slot - 1]]
        if slot in weights_end:
            ended.append(weights[weights_end[slot]][1])
        held.append(across(after(held[parent], ended), bits, ep_count))
    first = 0
    if paired:
        first = 1
        spare = [0 in bits for _, *bits in plan].index(True) + 1
        held[spare] = jnp.where(core == 1, own, held[spare])

    ids = jnp.stack([core * local_experts + place, (1 - core) * local_experts + place]).astype(jnp.int32)
    router_t = jnp.pad(router_w.T, ((0, -expert_count % 16), (0, 0)))
    done, late = (), held
    if paired:
        *done, own_gate, own_up, own_down = early(ids, held[1 : 1 + EARLY], router_t, *weights)
        weights = [(w, pair[1]) for w, pair in zip((own_gate, own_up, own_down), weights)]
        late = held[1 + EARLY :]
    outs = experts(ids, late, done, router_t, *weights)

    terms = {slot: [value] for slot, value in enumerate(outs, first)}
    if paired:
        terms[0] = [jnp.where(core == 1, outs[spare - 1], jnp.zeros_like(outs[spare - 1]))]

    def summed(slot):
        return sum(term.astype(jnp.float32) for term in terms[slot])

    returned = []
    for slot, (parent, *bits) in return_plan:
        value = summed(slot).astype(jnp.bfloat16)
        value = after(value, returned[: max(0, len(returned) + 1 - OPEN_RETURN)])
        returned.append(across(value, bits, ep_count))
        terms[parent].append(returned[-1])
    total = summed(0)
    if paired:
        arrived = between_cores(total[rows:].astype(jnp.bfloat16))
        total = total[:rows] + arrived.astype(jnp.float32)
    return total.astype(jnp.bfloat16)


def solution(mesh):
    in_specs = (
        P(("dom", "ep", "grp"), None),
        P(),
        P(),
        P(("dom", "ep", "grp"), None),
        P("ep", "grp", None, None),
        P("ep", "grp", None, None),
        P("ep", "grp", None, None),
    )
    out_specs = P(("dom", "ep", "grp"), None)
    return jax.shard_map(local, mesh=mesh, in_specs=in_specs, out_specs=out_specs, check_vma=False)
```

```python
import functools

import jax
import jax.numpy as jnp
from jax import lax
from jax.experimental import pallas as pl
from jax.experimental.pallas import tpu as pltpu
from jax.sharding import PartitionSpec as P

SPLIT = 4
LANES = 128

EPSILON = 1e-06
ROUTE_SCALE = 2.5
PREPARE_VMEM = 60 * 1024 * 1024
EXPERTS_VMEM = 16 * 1024 * 1024
EARLY_VMEM = 32 * 1024 * 1024

PLAN_16 = ((0, 1, 2), (0, 8, 4), (2, 4, 1), (2, 2, 2), (2, 1, 0), (3, 1, 2), (4, 1, 8), (6, 2, 4))
RETURN_16 = tuple((slot, PLAN_16[slot - 1]) for slot in (8, 7, 6, 4, 5, 3, 2, 1))
OPEN_16 = (2, 2, 2, 2, 2, 3, 4, 4)
WEIGHTS_END_16 = {6: 0, 7: 1}
OPEN_RETURN = 4
EARLY = 4


def plan_for(ep_count, grp_count):
    if ep_count == 16 and grp_count == 2:
        return PLAN_16, RETURN_16, OPEN_16, WEIGHTS_END_16, True
    plan = []
    for r in range(1, ep_count):
        bit = 1 << (r.bit_length() - 1)
        plan.append((r ^ bit, bit, bit))
    slots = len(plan)
    back = tuple((slot, plan[slot - 1]) for slot in range(slots, 0, -1))
    return tuple(plan), back, (OPEN_RETURN,) * slots, {}, False


def across(value, bits, ep_count):
    pairs = [(i * 2 + c, (i ^ bit) * 2 + c) for c, bit in enumerate(bits) if bit for i in range(ep_count)]
    return lax.ppermute(value, ("ep", "grp"), pairs)


def after(value, earlier):
    return lax.optimization_barrier((value, *earlier))[0] if earlier else value


def between_cores(value):
    return lax.ppermute(value, "grp", [(0, 1), (1, 0)])


def prepare_kernel(count, *refs):
    sources, out_ref, targets, sems = refs[: 2 * count + 1], refs[2 * count + 1], refs[2 * count + 2 : -1], refs[-1]
    copies = [
        pltpu.make_async_copy(source, target, sems.at[i]) for i, (source, target) in enumerate(zip(sources, targets))
    ]
    for copy in copies:
        copy.start()
    for copy in copies:
        copy.wait()
    gain = targets[0][...]
    for i in range(count):
        values = targets[1 + i][...].astype(jnp.float32)
        routes = targets[1 + count + i][...]
        rows, width = values.shape
        span = pl.ds(i * rows, rows)
        square_mean = jnp.mean(values * values, axis=1, keepdims=True)
        normed = values * lax.rsqrt(square_mean + EPSILON) * gain
        out_ref[span, :width] = normed.astype(jnp.bfloat16)
        experts_down = lax.broadcasted_iota(jnp.int32, (LANES, rows), 0)
        named = jnp.zeros((LANES, rows), jnp.float32)
        for k in range(routes.shape[0]):
            named = jnp.where(experts_down == routes[k : k + 1, :], 1.0, named)
        same = lax.broadcasted_iota(jnp.int32, (rows, rows), 0) == lax.broadcasted_iota(jnp.int32, (rows, rows), 1)
        out_ref[span, width:] = lax.dot_general(
            same.astype(jnp.bfloat16),
            named.astype(jnp.bfloat16),
            (((1,), (1,)), ((), ())),
            preferred_element_type=jnp.float32,
        ).astype(jnp.bfloat16)


def prepare(gain, hiddens, routes):
    rows, width = hiddens[0].shape
    count = len(hiddens)
    operands = (gain[None, :], *hiddens, *routes)
    return pl.pallas_call(
        functools.partial(prepare_kernel, count),
        out_shape=jax.ShapeDtypeStruct((count * rows, width + LANES), jnp.bfloat16),
        in_specs=[pl.BlockSpec(memory_space=pl.ANY)] * len(operands),
        scratch_shapes=[pltpu.VMEM(x.shape, x.dtype) for x in operands] + [pltpu.SemaphoreType.DMA((len(operands),))],
        compiler_params=pltpu.CompilerParams(vmem_limit_bytes=PREPARE_VMEM),
        cost_estimate=pl.CostEstimate(
            flops=6 * count * rows * width, bytes_accessed=4 * count * rows * width, transcendentals=count * rows
        ),
        name="prepare",
    )(*operands)


def gate_up(ids_ref, token_refs, router_ref, weight_refs, tokens_ref, copies=()):
    rows = token_refs[0].shape[0]
    width = weight_refs[0].shape[0]
    for i, ref in enumerate(token_refs):
        tokens_ref[i * rows : (i + 1) * rows, :] = ref[...]

    def product(ref):
        return jnp.dot(tokens_ref[:, :width], ref[...], preferred_element_type=jnp.float32)

    logits = lax.dot_general(
        tokens_ref[:, :width], router_ref[...], (((1,), (1,)), ((), ())), preferred_element_type=jnp.float32
    )
    named = tokens_ref[:, width:][:, : logits.shape[1]].astype(jnp.float32)
    chosen = named * jax.nn.sigmoid(logits)
    weights = ROUTE_SCALE * chosen / jnp.sum(chosen, axis=1, keepdims=True)
    lanes = lax.broadcasted_iota(jnp.int32, weights.shape, 1)
    acts, columns = [None, None], []
    for i in (1, 0):
        if i == 0:
            for copy in copies:
                copy.wait()
        acts[i] = (jax.nn.silu(product(weight_refs[i])) * product(weight_refs[2 + i])).astype(jnp.bfloat16)
    for i in range(2):
        column = jnp.sum(jnp.where(lanes == ids_ref[i], weights, 0.0), axis=1, keepdims=True)
        columns.append(jnp.broadcast_to(column, (column.shape[0], LANES)))
    return jnp.concatenate(acts, axis=1), jnp.concatenate(columns, axis=1)


def early_kernel(blocks, ids_ref, *refs):
    token_refs, router_ref = refs[:blocks], refs[blocks]
    gate1_ref, up1_ref, *own_hbm = refs[blocks + 1 : blocks + 6]
    act_ref, coeff_ref, *own_refs, tokens_ref, sems = refs[blocks + 6 :]
    copies = [
        pltpu.make_async_copy(source, target, sems.at[i]) for i, (source, target) in enumerate(zip(own_hbm, own_refs))
    ]
    for copy in copies:
        copy.start()
    weight_refs = (own_refs[0], gate1_ref, own_refs[1], up1_ref)
    act_ref[...], coeff_ref[...] = gate_up(ids_ref, token_refs, router_ref, weight_refs, tokens_ref, copies[:2])
    copies[2].wait()


def early(ids, token_blocks, router_t, gates, ups, downs):
    blocks = len(token_blocks)
    width, hidden_units = gates[0].shape
    rows = blocks * token_blocks[0].shape[0]
    in_vmem = pl.BlockSpec(memory_space=pltpu.VMEM)
    own = (gates[0], ups[0], downs[0])
    return pl.pallas_call(
        functools.partial(early_kernel, blocks),
        in_specs=[pl.BlockSpec(memory_space=pltpu.SMEM)]
        + [in_vmem] * (blocks + 3)
        + [pl.BlockSpec(memory_space=pl.ANY)] * 3,
        out_specs=[in_vmem] * 5,
        out_shape=[
            jax.ShapeDtypeStruct((rows, 2 * hidden_units), jnp.bfloat16),
            jax.ShapeDtypeStruct((rows, 2 * LANES), jnp.float32),
        ]
        + [jax.ShapeDtypeStruct(w.shape, w.dtype) for w in own],
        scratch_shapes=[pltpu.VMEM((rows, width + LANES), jnp.bfloat16), pltpu.SemaphoreType.DMA((3,))],
        compiler_params=pltpu.CompilerParams(vmem_limit_bytes=EARLY_VMEM),
        cost_estimate=pl.CostEstimate(
            flops=8 * rows * width * hidden_units,
            bytes_accessed=8 * width * hidden_units + 2 * rows * width,
            transcendentals=2 * rows * hidden_units,
        ),
        name="early",
    )(ids, *token_blocks, router_t, gates[1], ups[1], *own)


def experts_kernel(blocks, done_rows, rows, n_tile, ids_ref, *refs):
    token_refs, router_ref = refs[:blocks], refs[blocks]
    weight_refs, down0_ref, down1_ref = refs[blocks + 1 : blocks + 5], refs[blocks + 5], refs[blocks + 6]
    refs = refs[blocks + 7 :]
    if done_rows:
        done_act_ref, done_coeff_ref, *refs = refs
    *out_refs, tokens_ref, act_ref, coeff_ref = refs
    hidden_units, width = down0_ref.shape
    act, coeff = gate_up(ids_ref, token_refs, router_ref, weight_refs, tokens_ref)
    act_ref[done_rows:, :] = act
    coeff_ref[done_rows:, :] = coeff
    if done_rows:
        act_ref[:done_rows, :] = done_act_ref[...]
        coeff_ref[:done_rows, :] = done_coeff_ref[...]
    for j in range(width // n_tile):
        span = slice(j * n_tile, (j + 1) * n_tile)
        total = coeff_ref[:, 0:1] * jnp.dot(
            act_ref[:, :hidden_units], down0_ref[:, span], preferred_element_type=jnp.float32
        ) + coeff_ref[:, LANES : LANES + 1] * jnp.dot(
            act_ref[:, hidden_units:], down1_ref[:, span], preferred_element_type=jnp.float32
        )
        for i, ref in enumerate(out_refs):
            ref[:, span] = total[i * rows : (i + 1) * rows].astype(jnp.bfloat16)


def experts(ids, token_blocks, done, router_t, gates, ups, downs):
    blocks = len(token_blocks)
    rows = token_blocks[0].shape[0]
    width, hidden_units = gates[0].shape
    late_rows = blocks * rows
    done_rows = done[0].shape[0] if done else 0
    all_rows = done_rows + late_rows
    outs = all_rows // rows
    in_vmem = pl.BlockSpec(memory_space=pltpu.VMEM)
    return pl.pallas_call(
        functools.partial(experts_kernel, blocks, done_rows, rows, 1024),
        in_specs=[pl.BlockSpec(memory_space=pltpu.SMEM)] + [in_vmem] * (blocks + 7 + len(done)),
        out_specs=[in_vmem] * outs,
        out_shape=[jax.ShapeDtypeStruct((rows, width), jnp.bfloat16)] * outs,
        scratch_shapes=[
            pltpu.VMEM((late_rows, width + LANES), jnp.bfloat16),
            pltpu.VMEM((all_rows, 2 * hidden_units), jnp.bfloat16),
            pltpu.VMEM((all_rows, 2 * LANES), jnp.float32),
        ],
        compiler_params=pltpu.CompilerParams(vmem_limit_bytes=EXPERTS_VMEM),
        cost_estimate=pl.CostEstimate(
            flops=(8 * late_rows + 4 * all_rows) * width * hidden_units,
            bytes_accessed=12 * width * hidden_units + 4 * all_rows * width,
            transcendentals=2 * late_rows * hidden_units,
        ),
        name="experts",
    )(ids, *token_blocks, router_t, *gates, *ups, *downs, *done)


def local(hidden, gain, router_w, routes, w_gate, w_up, w_down):
    ep_count, grp_count = lax.axis_size("ep"), lax.axis_size("grp")
    local_experts = ep_count // SPLIT
    expert_count = local_experts * grp_count
    place, core = lax.axis_index("ep") // SPLIT, lax.axis_index("grp")
    plan, return_plan, most_open, weights_end, paired = plan_for(ep_count, grp_count)
    rows = hidden.shape[0]
    hiddens, chosen = [hidden], [routes.T]
    if paired:
        hiddens.append(between_cores(hidden))
        chosen.append(between_cores(routes.T))
    own = prepare(gain, hiddens, chosen)
    weights = [(w[0, 0], between_cores(after(w[0, 0], hiddens[1:] + chosen[1:]))) for w in (w_gate, w_up, w_down)]
    held = [own]
    for slot, (parent, *bits) in enumerate(plan, 1):
        ended = held[1 : slot + 1 - most_open[slot - 1]]
        if slot in weights_end:
            ended.append(weights[weights_end[slot]][1])
        held.append(across(after(held[parent], ended), bits, ep_count))
    first = 0
    if paired:
        first = 1
        spare = [0 in bits for _, *bits in plan].index(True) + 1
        held[spare] = jnp.where(core == 1, own, held[spare])

    ids = jnp.stack([core * local_experts + place, (1 - core) * local_experts + place]).astype(jnp.int32)
    router_t = jnp.pad(router_w.T, ((0, -expert_count % 16), (0, 0)))
    done, late = (), held
    if paired:
        *done, own_gate, own_up, own_down = early(ids, held[1 : 1 + EARLY], router_t, *weights)
        weights = [(w, pair[1]) for w, pair in zip((own_gate, own_up, own_down), weights)]
        late = held[1 + EARLY :]
    outs = experts(ids, late, done, router_t, *weights)

    terms = {slot: [value] for slot, value in enumerate(outs, first)}
    if paired:
        terms[0] = [jnp.where(core == 1, outs[spare - 1], jnp.zeros_like(outs[spare - 1]))]

    def summed(slot):
        return sum(term.astype(jnp.float32) for term in terms[slot])

    returned = []
    for slot, (parent, *bits) in return_plan:
        value = summed(slot).astype(jnp.bfloat16)
        value = after(value, returned[: max(0, len(returned) + 1 - OPEN_RETURN)])
        returned.append(across(value, bits, ep_count))
        terms[parent].append(returned[-1])
    total = summed(0)
    if paired:
        arrived = between_cores(total[rows:].astype(jnp.bfloat16))
        total = total[:rows] + arrived.astype(jnp.float32)
    return total.astype(jnp.bfloat16)


def solution(mesh):
    in_specs = (
        P(("dom", "ep", "grp"), None),
        P(),
        P(),
        P(("dom", "ep", "grp"), None),
        P("ep", "grp", None, None),
        P("ep", "grp", None, None),
        P("ep", "grp", None, None),
    )
    out_specs = P(("dom", "ep", "grp"), None)
    return jax.shard_map(local, mesh=mesh, in_specs=in_specs, out_specs=out_specs, check_vma=False)
```

```python
import functools

import jax
import jax.numpy as jnp
from jax import lax
from jax.experimental import pallas as pl
from jax.experimental.pallas import tpu as pltpu
from jax.sharding import PartitionSpec as P

SPLIT = 4
LANES = 128

EPSILON = 1e-06
ROUTE_SCALE = 2.5
PREPARE_VMEM = 60 * 1024 * 1024
EXPERTS_VMEM = 47 * 1024 * 1024

PLAN_16 = ((0, 1, 2), (0, 8, 4), (2, 4, 1), (2, 2, 2), (2, 1, 0), (3, 1, 2), (4, 1, 8), (6, 2, 4))
RETURN_16 = tuple((slot, PLAN_16[slot - 1]) for slot in (8, 7, 6, 4, 5, 3, 2, 1))
OPEN_16 = (2, 2, 2, 2, 2, 3, 4, 4)
WEIGHTS_END_16 = {6: 0, 7: 1}
OPEN_RETURN = 4
EARLY = 5


def plan_for(ep_count, grp_count):
    if ep_count == 16 and grp_count == 2:
        return PLAN_16, RETURN_16, OPEN_16, WEIGHTS_END_16, True
    plan = []
    for r in range(1, ep_count):
        bit = 1 << (r.bit_length() - 1)
        plan.append((r ^ bit, bit, bit))
    slots = len(plan)
    back = tuple((slot, plan[slot - 1]) for slot in range(slots, 0, -1))
    return tuple(plan), back, (OPEN_RETURN,) * slots, {}, False


def across(value, bits, ep_count):
    pairs = [(i * 2 + c, (i ^ bit) * 2 + c) for c, bit in enumerate(bits) for i in range(ep_count)]
    return lax.ppermute(value, ("ep", "grp"), pairs)


def after(value, earlier):
    return lax.optimization_barrier((value, *earlier))[0] if earlier else value


def between_cores(value):
    return lax.ppermute(value, "grp", [(0, 1), (1, 0)])


def prepare_kernel(count, *refs):
    sources, out_ref, targets, sems = refs[: 2 * count + 1], refs[2 * count + 1], refs[2 * count + 2 : -1], refs[-1]
    copies = [
        pltpu.make_async_copy(source, target, sems.at[i]) for i, (source, target) in enumerate(zip(sources, targets))
    ]
    for copy in copies:
        copy.start()
    for copy in copies:
        copy.wait()
    gain = targets[0][...]
    for i in range(count):
        values = targets[1 + i][...].astype(jnp.float32)
        routes = targets[1 + count + i][...]
        rows, width = values.shape
        span = pl.ds(i * rows, rows)
        square_mean = jnp.mean(values * values, axis=1, keepdims=True)
        normed = values * lax.rsqrt(square_mean + EPSILON) * gain
        out_ref[span, :width] = normed.astype(jnp.bfloat16)
        experts_down = lax.broadcasted_iota(jnp.int32, (LANES, rows), 0)
        named = jnp.zeros((LANES, rows), jnp.float32)
        for k in range(routes.shape[0]):
            named = jnp.where(experts_down == routes[k : k + 1, :], 1.0, named)
        same = lax.broadcasted_iota(jnp.int32, (rows, rows), 0) == lax.broadcasted_iota(jnp.int32, (rows, rows), 1)
        out_ref[span, width:] = lax.dot_general(
            same.astype(jnp.bfloat16),
            named.astype(jnp.bfloat16),
            (((1,), (1,)), ((), ())),
            preferred_element_type=jnp.float32,
        ).astype(jnp.bfloat16)


def prepare(gain, hiddens, routes):
    rows, width = hiddens[0].shape
    count = len(hiddens)
    operands = (gain[None, :], *hiddens, *routes)
    return pl.pallas_call(
        functools.partial(prepare_kernel, count),
        out_shape=jax.ShapeDtypeStruct((count * rows, width + LANES), jnp.bfloat16),
        in_specs=[pl.BlockSpec(memory_space=pl.ANY)] * len(operands),
        scratch_shapes=[pltpu.VMEM(x.shape, x.dtype) for x in operands] + [pltpu.SemaphoreType.DMA((len(operands),))],
        compiler_params=pltpu.CompilerParams(vmem_limit_bytes=PREPARE_VMEM),
        cost_estimate=pl.CostEstimate(
            flops=6 * count * rows * width, bytes_accessed=4 * count * rows * width, transcendentals=count * rows
        ),
        name="prepare",
    )(*operands)


def add_products(step, k_tile, token_refs, router_ref, weight_refs, gates_ref, logits_ref):
    hidden_units = weight_refs[0].shape[1]
    columns = pl.ds(pl.multiple_of(step * k_tile, LANES), k_tile)
    tokens = jnp.concatenate([ref[:, columns] for ref in token_refs], axis=0)
    parts = [jnp.dot(tokens, ref[...], preferred_element_type=jnp.float32) for ref in weight_refs]
    logits = lax.dot_general(
        tokens, router_ref[...], (((1,), (1,)), ((), ())), preferred_element_type=jnp.float32
    )

    @pl.when(step == 0)
    def _():
        for i, part in enumerate(parts):
            gates_ref[:, i * hidden_units : (i + 1) * hidden_units] = part
        logits_ref[...] = logits

    @pl.when(step > 0)
    def _():
        for i, part in enumerate(parts):
            gates_ref[:, i * hidden_units : (i + 1) * hidden_units] += part
        logits_ref[...] += logits


def activate(width, ids_ref, token_refs, gates_ref, logits_ref):
    half = gates_ref.shape[1] // 2
    act = (jax.nn.silu(gates_ref[:, :half]) * gates_ref[:, half:]).astype(jnp.bfloat16)
    named = jnp.concatenate([ref[:, width : width + LANES] for ref in token_refs], axis=0)
    chosen = named[:, : logits_ref.shape[1]].astype(jnp.float32) * jax.nn.sigmoid(logits_ref[...])
    weights = ROUTE_SCALE * chosen / jnp.sum(chosen, axis=1, keepdims=True)
    lanes = lax.broadcasted_iota(jnp.int32, weights.shape, 1)
    columns = []
    for i in range(2):
        column = jnp.sum(jnp.where(lanes == ids_ref[i], weights, 0.0), axis=1, keepdims=True)
        columns.append(jnp.broadcast_to(column, (column.shape[0], LANES)))
    return act, jnp.concatenate(columns, axis=1)


def early_kernel(blocks, k_steps, k_tile, ids_ref, *refs):
    token_refs, router_ref, weight_refs = refs[:blocks], refs[blocks], refs[blocks + 1 : blocks + 5]
    act_ref, coeff_ref, gates_ref, logits_ref = refs[blocks + 5 :]
    step = pl.program_id(0)
    add_products(step, k_tile, token_refs, router_ref, weight_refs, gates_ref, logits_ref)

    @pl.when(step == k_steps - 1)
    def _():
        act_ref[...], coeff_ref[...] = activate(k_steps * k_tile, ids_ref, token_refs, gates_ref, logits_ref)


def early(ids, token_blocks, router_t, gates, ups):
    blocks = len(token_blocks)
    width, hidden_units = gates[0].shape
    rows = blocks * token_blocks[0].shape[0]
    k_steps = 4
    k_tile = width // k_steps
    return pl.pallas_call(
        functools.partial(early_kernel, blocks, k_steps, k_tile),
        grid_spec=pltpu.PrefetchScalarGridSpec(
            num_scalar_prefetch=1,
            grid=(k_steps,),
            in_specs=[pl.BlockSpec(token_blocks[0].shape, lambda step, ids_ref: (0, 0))] * blocks
            + [pl.BlockSpec((router_t.shape[0], k_tile), lambda step, ids_ref: (0, step))]
            + [pl.BlockSpec((k_tile, hidden_units), lambda step, ids_ref: (step, 0))] * 4,
            out_specs=[
                pl.BlockSpec((rows, 2 * hidden_units), lambda step, ids_ref: (0, 0)),
                pl.BlockSpec((rows, 2 * LANES), lambda step, ids_ref: (0, 0)),
            ],
            scratch_shapes=[
                pltpu.VMEM((rows, 4 * hidden_units), jnp.float32),
                pltpu.VMEM((rows, router_t.shape[0]), jnp.float32),
            ],
        ),
        out_shape=[
            jax.ShapeDtypeStruct((rows, 2 * hidden_units), jnp.bfloat16),
            jax.ShapeDtypeStruct((rows, 2 * LANES), jnp.float32),
        ],
        compiler_params=pltpu.CompilerParams(vmem_limit_bytes=EXPERTS_VMEM),
        cost_estimate=pl.CostEstimate(
            flops=8 * rows * width * hidden_units,
            bytes_accessed=8 * width * hidden_units + 2 * rows * width,
            transcendentals=2 * rows * hidden_units,
        ),
        name="early",
    )(ids, *token_blocks, router_t, *gates, *ups)


def experts_kernel(blocks, done_rows, rows, k_steps, k_tile, ids_ref, *refs):
    token_refs, router_ref = refs[:blocks], refs[blocks]
    weight_refs, down0_ref, down1_ref = refs[blocks + 1 : blocks + 5], refs[blocks + 5], refs[blocks + 6]
    refs = refs[blocks + 7 :]
    if done_rows:
        done_act_ref, done_coeff_ref, *refs = refs
    *out_refs, gates_ref, logits_ref, act_ref, coeff_ref = refs
    hidden_units = weight_refs[0].shape[1]
    step = pl.program_id(0)

    @pl.when(step < k_steps)
    def _():
        add_products(step, k_tile, token_refs, router_ref, weight_refs, gates_ref, logits_ref)

    @pl.when(step == k_steps - 1)
    def _():
        act, coeff = activate(k_steps * k_tile, ids_ref, token_refs, gates_ref, logits_ref)
        act_ref[done_rows:, :] = act
        coeff_ref[done_rows:, :] = coeff
        if done_rows:
            act_ref[:done_rows, :] = done_act_ref[...]
            coeff_ref[:done_rows, :] = done_coeff_ref[...]

    @pl.when(step >= k_steps)
    def _():
        total = coeff_ref[:, 0:1] * jnp.dot(
            act_ref[:, :hidden_units], down0_ref[...], preferred_element_type=jnp.float32
        ) + coeff_ref[:, LANES : LANES + 1] * jnp.dot(
            act_ref[:, hidden_units:], down1_ref[...], preferred_element_type=jnp.float32
        )
        for i, ref in enumerate(out_refs):
            ref[...] = total[i * rows : (i + 1) * rows].astype(jnp.bfloat16)


def experts(ids, token_blocks, done, router_t, gates, ups, downs):
    blocks = len(token_blocks)
    rows = token_blocks[0].shape[0]
    width, hidden_units = gates[0].shape
    k_steps = n_steps = 4
    k_tile, n_tile = width // k_steps, width // n_steps
    late_rows = blocks * rows
    done_rows = done[0].shape[0] if done else 0
    all_rows = done_rows + late_rows
    outs = all_rows // rows

    def at_k(step):
        return jnp.minimum(step, k_steps - 1)

    def at_n(step):
        return jnp.maximum(step - k_steps, 0)

    in_specs = [pl.BlockSpec(token_blocks[0].shape, lambda step, ids_ref: (0, 0))] * blocks
    in_specs += [pl.BlockSpec((router_t.shape[0], k_tile), lambda step, ids_ref: (0, at_k(step)))]
    in_specs += [pl.BlockSpec((k_tile, hidden_units), lambda step, ids_ref: (at_k(step), 0))] * 4
    in_specs += [pl.BlockSpec((hidden_units, n_tile), lambda step, ids_ref: (0, at_n(step)))] * 2
    in_specs += [pl.BlockSpec(x.shape, lambda step, ids_ref: (0, 0)) for x in done]
    return pl.pallas_call(
        functools.partial(experts_kernel, blocks, done_rows, rows, k_steps, k_tile),
        grid_spec=pltpu.PrefetchScalarGridSpec(
            num_scalar_prefetch=1,
            grid=(k_steps + n_steps,),
            in_specs=in_specs,
            out_specs=[pl.BlockSpec((rows, n_tile), lambda step, ids_ref: (0, at_n(step)))] * outs,
            scratch_shapes=[
                pltpu.VMEM((late_rows, 4 * hidden_units), jnp.float32),
                pltpu.VMEM((late_rows, router_t.shape[0]), jnp.float32),
                pltpu.VMEM((all_rows, 2 * hidden_units), jnp.bfloat16),
                pltpu.VMEM((all_rows, 2 * LANES), jnp.float32),
            ],
        ),
        out_shape=[jax.ShapeDtypeStruct((rows, width), jnp.bfloat16)] * outs,
        compiler_params=pltpu.CompilerParams(vmem_limit_bytes=EXPERTS_VMEM),
        cost_estimate=pl.CostEstimate(
            flops=(8 * late_rows + 4 * all_rows) * width * hidden_units,
            bytes_accessed=12 * width * hidden_units + 4 * all_rows * width,
            transcendentals=2 * late_rows * hidden_units,
        ),
        name="experts",
    )(ids, *token_blocks, router_t, *gates, *ups, *downs, *done)


def local(hidden, gain, router_w, routes, w_gate, w_up, w_down):
    ep_count, grp_count = lax.axis_size("ep"), lax.axis_size("grp")
    local_experts = ep_count // SPLIT
    expert_count = local_experts * grp_count
    place, core = lax.axis_index("ep") // SPLIT, lax.axis_index("grp")
    plan, return_plan, most_open, weights_end, paired = plan_for(ep_count, grp_count)
    rows = hidden.shape[0]
    hiddens, chosen = [hidden], [routes.T]
    if paired:
        hiddens.append(between_cores(hidden))
        chosen.append(between_cores(routes.T))
    own = prepare(gain, hiddens, chosen)
    weights = [(w[0, 0], between_cores(after(w[0, 0], hiddens[1:] + chosen[1:]))) for w in (w_gate, w_up, w_down)]
    router_t = jnp.pad(router_w.T, ((0, -expert_count % 16), (0, 0)))
    held = [own]
    for slot, (parent, *bits) in enumerate(plan, 1):
        ended = held[1 : slot + 1 - most_open[slot - 1]]
        if slot in weights_end:
            ended.append(weights[weights_end[slot]][1])
        if paired and slot == 3:
            ended.append(router_t)
        held.append(across(after(held[parent], ended), bits, ep_count))
    first = 0
    if paired:
        first = 1
        spare = [0 in bits for _, *bits in plan].index(True) + 1
        held[spare] = jnp.where(core == 1, own, held[spare])

    ids = jnp.stack([core * local_experts + place, (1 - core) * local_experts + place]).astype(jnp.int32)
    done = early(ids, held[1 : 1 + EARLY], router_t, *weights[:2]) if paired else ()
    outs = experts(ids, held[1 + EARLY :] if paired else held, done, router_t, *weights)

    terms = {slot: [value] for slot, value in enumerate(outs, first)}
    if paired:
        terms[0] = [jnp.where(core == 1, outs[spare - 1], jnp.zeros_like(outs[spare - 1]))]

    def summed(slot):
        return sum(term.astype(jnp.float32) for term in terms[slot])

    returned = []
    for slot, (parent, *bits) in return_plan:
        value = summed(slot).astype(jnp.bfloat16)
        if paired and slot == spare:
            value = jnp.where(core == 1, jnp.zeros_like(value), value)
        value = after(value, returned[: max(0, len(returned) + 1 - OPEN_RETURN)])
        returned.append(across(value, bits, ep_count))
        terms[parent].append(returned[-1])
    total = summed(0)
    if paired:
        arrived = between_cores(total[rows:].astype(jnp.bfloat16))
        total = total[:rows] + arrived.astype(jnp.float32)
    return total.astype(jnp.bfloat16)


def solution(mesh):
    in_specs = (
        P(("dom", "ep", "grp"), None),
        P(),
        P(),
        P(("dom", "ep", "grp"), None),
        P("ep", "grp", None, None),
        P("ep", "grp", None, None),
        P("ep", "grp", None, None),
    )
    out_specs = P(("dom", "ep", "grp"), None)
    return jax.shard_map(local, mesh=mesh, in_specs=in_specs, out_specs=out_specs, check_vma=False)
```
